128 devices in a mesh: band: 8 (over x, core), fft: 16 (over y, z).
Axes of the slice: x: 4, y: 4, z: 4, core: 2. Of those that a mesh axis runs over, the one named last changes fastest.
Arguments:
- orbitals: bfloat16 [16, 30720, 480], P('band', 'fft'), may hold values from -24 to 24
- potential: float32 [240, 57600], P('fft'), may hold values from -8 to 8
- stick_column: int32 [30720], replicated, may hold values from -1 to 57599, as said below
- column_slot: int32 [57600], replicated, may hold values from -1 to 30719, as said below
Outputs:
- applied_orbitals: bfloat16 [16, 30720, 480], P('band', 'fft')
- intersection: float32 [2, 16, 16], replicated
- hamiltonian: float32 [2, 16, 16], replicated
The draws below stay inside these ranges and needn't reach their ends.
Inputs may be any that keep to these rules, and one draw needn't show every extreme that they name: `stick_column`: the live entries are the 24576 flat indices x 240 + y of a disk of columns around zero wrapped frequency, each once; the slots p * 1920 to (p + 1) * 1920 - 1 of fft index p hold its sticks first, then -1; counts differ between indices and some index has all 1920 slots live. column_slot[stick_column[g]] = g for every live slot g, and -1 at every other flat index.
All inputs are finite; a program needn't handle non-finite values.
Results may differ from the reference program's by a relative error of at most 0.011.
Values may be sent and summed in bfloat16 or wider, within the bound.
No kernel may reach another device: no remote copies, remote signals or barrier semaphores. Data moves between devices by JAX's collectives and lax.ppermute only.
A program may use at most 192 MiB of HBM per device.

```python
import math
import jax
import jax.numpy as jnp
import numpy as np
from jax import lax

GRID = 240
STICKS = 24576
NB = 16
SLOTS = 1920
N_FFT = 16


def disk_columns():
    frequency = np.arange(GRID)
    frequency = np.minimum(frequency, GRID - frequency)
    radius = frequency[:, None] ** 2 + frequency[None, :] ** 2
    ordering = np.argsort(radius.reshape(-1), kind='stable')
    return jnp.asarray(ordering[:STICKS].astype(np.int32))


def stick_layout(key):
    columns = disk_columns()
    shuffled = columns[jax.random.permutation(jax.random.fold_in(key, 11), STICKS)]
    fullest = jax.random.randint(jax.random.fold_in(key, 12), (), 0, N_FFT)
    weights = jax.random.randint(jax.random.fold_in(key, 13), (N_FFT,), 4, 6)
    devices = jnp.arange(N_FFT, dtype=jnp.int32)
    weights = jnp.where(devices == fullest, 0, weights)
    ends = jnp.cumsum(weights) * (STICKS - SLOTS) // jnp.sum(weights)
    counts = ends - jnp.concatenate([jnp.zeros((1,), jnp.int32), ends[:-1]])
    counts = jnp.where(devices == fullest, SLOTS, counts)
    offsets = jnp.cumsum(counts) - counts
    position = jnp.arange(STICKS, dtype=jnp.int32)
    owner = jnp.sum((offsets[None, :] <= position[:, None]).astype(jnp.int32), axis=1) - 1
    slot_index = owner * SLOTS + position - offsets[owner]
    stick_column = jnp.full((N_FFT * SLOTS,), -1, jnp.int32).at[slot_index].set(shuffled)
    column_slot = jnp.full((GRID * GRID,), -1, jnp.int32).at[shuffled].set(slot_index)
    return (stick_column, column_slot)


def band_modes(key):
    sign = jax.random.randint(jax.random.fold_in(key, 21), (NB,), 0, 2) * 2 - 1
    shift_x = sign * jax.random.randint(jax.random.fold_in(key, 22), (NB,), 1, 3)
    shift_y = jax.random.randint(jax.random.fold_in(key, 23), (NB,), -2, 3)
    shift_z = jax.random.randint(jax.random.fold_in(key, 24), (NB,), -2, 3)
    return (shift_x.astype(jnp.int32), shift_y.astype(jnp.int32), shift_z.astype(jnp.int32))


def draw_stick_column(key, part):
    return stick_layout(key)[0]


def draw_column_slot(key, part):
    return stick_layout(key)[1]


def draw_potential(key, part):
    shift_x, shift_y, shift_z = band_modes(key)
    key = jax.random.fold_in(key, 5)
    subkeys = jax.random.split(key, 3)
    cube = (GRID, GRID, GRID)
    amplitude = jax.random.uniform(subkeys[0], (NB,), jnp.float32, 0.6, 1.4) * (2.0 / math.sqrt(NB))
    rough = jnp.clip(jax.random.normal(subkeys[1], cube, jnp.float32) * 0.45, -2.0, 2.0)
    offset_angle = jax.random.uniform(subkeys[2], (NB,), jnp.float32, -math.pi, math.pi)
    plane_z = jnp.arange(GRID, dtype=jnp.int32)[:, None, None]
    plane_x = jnp.arange(GRID, dtype=jnp.int32)[None, :, None]
    plane_y = jnp.arange(GRID, dtype=jnp.int32)[None, None, :]

    def add_mode(index, total):
        steps = (shift_x[index] * plane_x + shift_y[index] * plane_y + shift_z[index] * plane_z) % GRID
        angle = steps.astype(jnp.float32) * (2.0 * math.pi / GRID) + offset_angle[index]
        return total + amplitude[index] * jnp.cos(angle)
    smooth = lax.fori_loop(0, NB, add_mode, jnp.zeros(cube, jnp.float32))
    return jnp.clip(smooth + rough, -8.0, 8.0).reshape(GRID, GRID * GRID)


def draw_orbitals(key, part):
    stick_column, column_slot = stick_layout(key)
    shift_x, shift_y, shift_z = band_modes(key)
    key = jax.random.fold_in(key, 7)
    subkeys = jax.random.split(key, 6)
    slot_total = N_FFT * SLOTS
    extent = (NB, slot_total, 2, GRID)
    single = jnp.clip(jax.random.normal(subkeys[0], extent, jnp.float32), -5.0, 5.0)
    shared = jnp.clip(jax.random.normal(subkeys[1], (slot_total, 2, GRID), jnp.float32), -5.0, 5.0)
    common = jnp.clip(jax.random.normal(subkeys[3], (slot_total, 2, GRID), jnp.float32), -5.0, 5.0)
    sign_flips = (jax.random.randint(subkeys[2], (NB, slot_total // 128, 1), 0, 2) * 2 - 1).astype(jnp.float32)
    sign_flips = jnp.broadcast_to(sign_flips, (NB, slot_total // 128, 128)).reshape(NB, slot_total, 1, 1)
    drawn_angle = jax.random.uniform(subkeys[4], (NB,), jnp.float32, -math.pi, math.pi)
    moved_angle = jax.random.uniform(subkeys[5], (NB,), jnp.float32, -math.pi, math.pi)
    rising = jnp.exp(jnp.arange(slot_total, dtype=jnp.float32) * (math.log(3.0) / slot_total))[:, None, None]
    common = common * rising
    base = shared * rising
    live = stick_column >= 0
    flat = jnp.maximum(stick_column, 0)
    column_x = flat // GRID
    column_y = flat % GRID
    frequency = jnp.arange(GRID, dtype=jnp.int32)

    def turn(values, angle):
        real_part = values[:, 0]
        imag_part = values[:, 1]
        cosine = jnp.cos(angle)
        sine = jnp.sin(angle)
        return jnp.stack([cosine * real_part - sine * imag_part, sine * real_part + cosine * imag_part], axis=1)

    def compose(items):
        single_band, flips, step_x, step_y, step_z, angle_drawn, angle_moved = items
        source = (column_x - step_x) % GRID * GRID + (column_y - step_y) % GRID
        source_slot = jnp.take(column_slot, source)
        usable = live & (source_slot >= 0)
        moved = jnp.take(common, jnp.maximum(source_slot, 0), axis=0)
        moved = jnp.take(moved, (frequency - step_z) % GRID, axis=2)
        moved = jnp.where(usable[:, None, None], moved, 0.0)
        total = rising * single_band + 0.6 * flips * base + 0.6 * (turn(common, angle_drawn) + turn(moved, angle_moved))
        return jnp.clip(total, -24.0, 24.0).reshape(slot_total, 2 * GRID).astype(jnp.bfloat16)
    return lax.map(compose, (single, sign_flips, shift_x, shift_y, shift_z, drawn_angle, moved_angle))


def setup_inputs(seed: int = 0) -> dict:
    key_of = jax.random.split(jax.random.key(seed), 5)
    orbitals = draw_orbitals(jax.random.fold_in(key_of[4], 71), 0)
    potential = draw_potential(jax.random.fold_in(key_of[4], 71), 0)
    stick_column = draw_stick_column(jax.random.fold_in(key_of[4], 71), 0)
    column_slot = draw_column_slot(jax.random.fold_in(key_of[4], 71), 0)
    return dict(orbitals=orbitals, potential=potential, stick_column=stick_column, column_slot=column_slot)


def fourier_tables(length, direction):
    counter = jnp.arange(length, dtype=jnp.int32)
    phases = counter[:, None] * counter[None, :] % length
    angles = phases.astype(jnp.float32) * (2.0 * math.pi / length)
    factor = 1.0 / math.sqrt(length)
    cosine = jnp.cos(angles) * factor
    sine = jnp.sin(angles) * (factor * direction)
    upper_half = jnp.stack([cosine, sine], axis=1)
    lower_half = jnp.stack([-sine, cosine], axis=1)
    return jnp.stack([upper_half, lower_half], axis=0).astype(jnp.bfloat16)

def rotated(values):
    middle = values.shape[-1] // 2
    return jnp.concatenate([values[..., middle:], -values[..., :middle]], axis=-1)

def reference(orbitals, potential, stick_column, column_slot):
    forward = fourier_tables(GRID, 1.0)
    backward = fourier_tables(GRID, -1.0)
    forward_wide = forward.astype(jnp.float32)
    backward_wide = backward.astype(jnp.float32)
    z_forward = forward.reshape(2 * GRID, 2 * GRID)
    z_backward = backward.reshape(2 * GRID, 2 * GRID)
    slot_total = N_FFT * SLOTS
    live_mask = (stick_column >= 0).astype(jnp.bfloat16)
    column_pick = jnp.maximum(stick_column, 0)
    slot_pick = jnp.maximum(column_slot, 0)
    filled = (column_slot >= 0)[None, None, :]
    field = potential.reshape(GRID, GRID, GRID)
    masked = orbitals * live_mask[None, :, None]

    def apply_band(coefs):
        zvalues = jnp.dot(coefs, z_forward, preferred_element_type=jnp.float32).astype(jnp.bfloat16)
        zplanes = zvalues.reshape(slot_total, 2, GRID).transpose(1, 2, 0)
        placed = jnp.where(filled, jnp.take(zplanes, slot_pick, axis=2), jnp.zeros((), jnp.bfloat16))
        placed = placed.reshape(2, GRID, GRID, GRID)
        sectioned = jnp.einsum('czxk,ckdy->dzxy', placed.astype(jnp.float32), forward_wide).astype(jnp.bfloat16)
        spatial = jnp.einsum('czky,ckdx->dzxy', sectioned.astype(jnp.float32), forward_wide)
        sectioned = (spatial * field[None]).astype(jnp.bfloat16)
        sectioned = jnp.einsum('czky,ckdx->dzxy', sectioned.astype(jnp.float32), backward_wide).astype(jnp.bfloat16)
        sectioned = jnp.einsum('czxk,ckdy->dzxy', sectioned.astype(jnp.float32), backward_wide).astype(jnp.bfloat16)
        picked = jnp.take(sectioned.reshape(2, GRID, GRID * GRID), column_pick, axis=2) * live_mask[None, None, :]
        sticks = picked.transpose(2, 0, 1).reshape(slot_total, 2 * GRID)
        result = jnp.dot(sticks, z_backward, preferred_element_type=jnp.float32)
        result = result * live_mask.astype(jnp.float32)[:, None]
        return result.astype(jnp.bfloat16)
    applied = lax.map(apply_band, masked)
    scale = 1.0 / (2.0 * STICKS * GRID)
    left = masked.reshape(NB, -1)
    turned = rotated(masked).reshape(NB, -1)
    right = applied.reshape(NB, -1)
    right_turned = rotated(applied).reshape(NB, -1)
    intersection = jnp.stack([jnp.dot(left, left.T, preferred_element_type=jnp.float32), jnp.dot(left, turned.T, preferred_element_type=jnp.float32)]) * scale
    hamiltonian = jnp.stack([jnp.dot(left, right.T, preferred_element_type=jnp.float32), jnp.dot(left, right_turned.T, preferred_element_type=jnp.float32)]) * scale
    return (applied, intersection, hamiltonian)
```

```python
import functools
import math

import jax
import jax.numpy as jnp
import ml_dtypes
import numpy as np
from jax import lax
from jax.experimental import pallas as pl
from jax.experimental.pallas import tpu as pltpu
from jax.sharding import PartitionSpec as P

STICKS = 24576
GRID = 240
SLOTS = 1920
GROUPS = 16
PLANES = 15
ZPAD = 16
BOX = 192
HALF = BOX // 2
PAIRS = GRID // 2
ROWS = BOX * BOX
BLOCK = 384
MIB = 1 << 20


def trig():
    counter = np.arange(GRID, dtype=np.int32)
    phases = counter[:, None] * counter[None, :] % GRID
    angles = phases.astype(np.float32) * np.float32(2.0 * math.pi / GRID)
    factor = np.float32(1.0 / math.sqrt(GRID))
    cosine = (np.cos(angles) * factor).astype(ml_dtypes.bfloat16)
    sine = (np.sin(angles) * factor).astype(ml_dtypes.bfloat16)
    return cosine, sine


def tables():
    cosine, sine = trig()
    box = np.arange(BOX) - HALF
    box = np.where(box < 0, box + GRID, box)
    z_forward = np.zeros((GROUPS, 2, ZPAD, 2, GRID), ml_dtypes.bfloat16)
    cos_z = cosine.reshape(GROUPS, PLANES, GRID)
    sin_z = sine.reshape(GROUPS, PLANES, GRID)
    z_forward[:, 0, :PLANES, 0] = cos_z
    z_forward[:, 0, :PLANES, 1] = -sin_z
    z_forward[:, 1, :PLANES, 0] = sin_z
    z_forward[:, 1, :PLANES, 1] = cos_z
    z_forward = z_forward.reshape(GROUPS * 2 * ZPAD, 2 * GRID)
    z_backward = np.ascontiguousarray(z_forward.T)
    cos_box, sin_box = cosine[:, box], sine[:, box]
    forward = np.concatenate([cos_box, sin_box], axis=1)
    backward = np.concatenate([cos_box.T, -sin_box.T], axis=1)
    return z_forward, z_backward, forward, backward


def z_forward_kernel(orbit_ref, live_ref, table_ref, wire_ref, share_ref):
    masked = (orbit_ref[0].astype(jnp.float32) * live_ref[...]).astype(jnp.bfloat16)
    values = jnp.dot(table_ref[...], masked, preferred_element_type=jnp.float32).astype(jnp.bfloat16)
    lanes = values.shape[-1]
    wire_ref[...] = values.reshape(GROUPS, 2, 1, ZPAD, lanes)
    for c in range(2):
        for q in range(15):
            share_ref[q // 2, q % 2, c, 0] = masked[c * GRID + q * 16 : c * GRID + q * 16 + 16]
        share_ref[7, 1, c, 0] = jnp.zeros((16, lanes), jnp.bfloat16)


def z_forward_call(orbits, live, table):
    lanes = BLOCK
    return pl.pallas_call(
        z_forward_kernel,
        grid=(2, SLOTS // lanes),
        in_specs=[
            pl.BlockSpec((1, 2 * GRID, lanes), lambda b, t: (b, 0, t)),
            pl.BlockSpec((1, lanes), lambda b, t: (0, t)),
            pl.BlockSpec((512, 2 * GRID), lambda b, t: (0, 0)),
        ],
        out_specs=[
            pl.BlockSpec((GROUPS, 2, 1, ZPAD, lanes), lambda b, t: (0, 0, b, 0, t)),
            pl.BlockSpec((8, 2, 2, 1, 16, lanes), lambda b, t: (0, 0, 0, b, 0, t)),
        ],
        out_shape=[
            jax.ShapeDtypeStruct((GROUPS, 2, 2, ZPAD, SLOTS), jnp.bfloat16),
            jax.ShapeDtypeStruct((8, 2, 2, 2, 16, SLOTS), jnp.bfloat16),
        ],
        compiler_params=pltpu.CompilerParams(vmem_limit_bytes=40 * MIB),
        cost_estimate=pl.CostEstimate(flops=1_800_000_000, bytes_accessed=12_000_000, transcendentals=0),
        name="z_forward",
    )(orbits, live, table)


def z_backward_kernel(wire_ref, live_ref, table_ref, out_ref):
    lanes = wire_ref.shape[-1]
    values = wire_ref[...].reshape(512, lanes)
    applied = jnp.dot(table_ref[...], values, preferred_element_type=jnp.float32)
    out_ref[0] = (applied * live_ref[...]).astype(jnp.bfloat16)


def z_backward_call(wire, live, table):
    lanes = BLOCK
    return pl.pallas_call(
        z_backward_kernel,
        grid=(2, SLOTS // lanes),
        in_specs=[
            pl.BlockSpec((GROUPS, 2, 1, ZPAD, lanes), lambda b, t: (0, 0, b, 0, t)),
            pl.BlockSpec((1, lanes), lambda b, t: (0, t)),
            pl.BlockSpec((2 * GRID, 512), lambda b, t: (0, 0)),
        ],
        out_specs=pl.BlockSpec((1, 2 * GRID, lanes), lambda b, t: (b, 0, t)),
        out_shape=jax.ShapeDtypeStruct((2, 2 * GRID, SLOTS), jnp.bfloat16),
        compiler_params=pltpu.CompilerParams(vmem_limit_bytes=40 * MIB),
        cost_estimate=pl.CostEstimate(flops=1_800_000_000, bytes_accessed=8_000_000, transcendentals=0),
        name="z_backward",
    )(wire, live, table)


def gram_kernel(left_ref, right_ref, out_ref, total):
    step = pl.program_id(0) * pl.num_programs(1) + pl.program_id(1)
    lanes = left_ref.shape[-1]
    left = left_ref[...].reshape(512, lanes)
    right = right_ref[...].reshape(512, lanes)
    product = lax.dot_general(left, right, (((1,), (1,)), ((), ())), preferred_element_type=jnp.float32)

    @pl.when(step == 0)
    def _():
        total[...] = product

    @pl.when(step > 0)
    def _():
        total[...] += product

    @pl.when(step == pl.num_programs(0) * pl.num_programs(1) - 1)
    def _():
        row = lax.broadcasted_iota(jnp.int32, (512, 512), 0)
        column = lax.broadcasted_iota(jnp.int32, (512, 512), 1)
        diagonal = jnp.where(row % 16 == column % 16, total[...], 0.0)
        pick_row = lax.broadcasted_iota(jnp.int32, (32, 512), 0)
        pick_column = lax.broadcasted_iota(jnp.int32, (32, 512), 1)
        pick = jnp.where(pick_column // 16 == pick_row, 1.0, 0.0)
        by_row = jnp.dot(pick, diagonal, preferred_element_type=jnp.float32, precision=lax.Precision.HIGHEST)
        out_ref[...] = lax.dot_general(
            by_row,
            pick,
            (((1,), (1,)), ((), ())),
            preferred_element_type=jnp.float32,
            precision=lax.Precision.HIGHEST,
        )


def gram_call(left, right, name):
    lanes = 640
    spec = pl.BlockSpec((8, 1, 2, 2, 16, lanes), lambda g, t: (0, g, 0, 0, 0, t))
    return pl.pallas_call(
        gram_kernel,
        grid=(2, SLOTS // lanes),
        in_specs=[spec, spec],
        out_specs=pl.BlockSpec((32, 32), lambda g, t: (0, 0)),
        out_shape=jax.ShapeDtypeStruct((32, 32), jnp.float32),
        scratch_shapes=[pltpu.VMEM((512, 512), jnp.float32)],
        compiler_params=pltpu.CompilerParams(vmem_limit_bytes=40 * MIB),
        cost_estimate=pl.CostEstimate(flops=2_000_000_000, bytes_accessed=8_000_000, transcendentals=0),
        name=name,
    )(left, right)


def matrices(product):
    parts = product.reshape(8, 2, 2, 8, 2, 2)
    first = parts[:, 0, :, :, 0, :] + parts[:, 1, :, :, 1, :]
    second = parts[:, 0, :, :, 1, :] - parts[:, 1, :, :, 0, :]
    return jnp.stack([first.reshape(16, 16), second.reshape(16, 16)])


def plane_kernel(
    place_ref, count_ref, wire_ref, field_ref, forward_ref, backward_ref, out_ref, grid_ref, mid_ref, stage_a, stage_b
):
    step = pl.program_id(0)
    lane = lax.broadcasted_iota(jnp.int32, (1, 128), 1)
    low = lane % 64 < 32
    sign = jnp.where(lane < 64, -1.0, 1.0)

    def turned(values):
        return pltpu.roll(values, 64, 1) * sign

    def doubled(values):
        return jnp.concatenate([values, turned(values)], axis=0).astype(jnp.bfloat16)

    def exchange(first, second):
        return (
            jnp.where(low, first, pltpu.roll(second, 32, 1)),
            jnp.where(low, pltpu.roll(first, 96, 1), second),
        )

    @pl.when(step == 0)
    def _():
        def clear(i, carry):
            grid_ref[pl.ds(pl.multiple_of(i * 512, 512), 512), :] = jnp.zeros((512, 128), jnp.float32)
            return carry

        lax.fori_loop(0, ROWS // 512, clear, 0)
        eye_row = lax.broadcasted_iota(jnp.int32, (128, 128), 0)
        eye_column = lax.broadcasted_iota(jnp.int32, (128, 128), 1)
        eye = jnp.where(eye_row == eye_column, 1.0, 0.0).astype(jnp.bfloat16)

        def group(p, carry):
            def scatter(t, inner):
                base = pl.multiple_of(t * 128, 128)
                block = wire_ref[p, :, pl.ds(base, 128)]
                twice = jnp.concatenate([block[0:32], block[0:32], block[32:64], block[32:64]], axis=0)
                stage_a[...] = lax.dot_general(
                    eye, twice, (((1,), (1,)), ((), ())), preferred_element_type=jnp.float32
                )
                first = p * SLOTS + base
                for u in range(128):
                    grid_ref[pl.ds(place_ref[first + u], 1), :] = stage_a[u : u + 1, :]
                return inner

            return lax.fori_loop(0, count_ref[p], scatter, carry)

        lax.fori_loop(0, GROUPS, group, 0)

        def x_forward(i, carry):
            parts = []
            for j in range(4):
                k = i * 4 + j
                first = grid_ref[pl.ds(pl.multiple_of(k * BOX, BOX), BOX), :]
                second = grid_ref[pl.ds(pl.multiple_of((k + HALF) * BOX, BOX), BOX), :]
                parts.append(doubled(jnp.where(low, first, second)))
            result = jnp.dot(forward_ref[...], jnp.concatenate(parts, axis=1), preferred_element_type=jnp.float32)
            for j in range(4):
                k = i * 4 + j
                part = result[:, j * 128 : (j + 1) * 128]
                mid_ref[pl.ds(k, PAIRS, stride=BOX), :] = part[:PAIRS]
                mid_ref[pl.ds(k + HALF, PAIRS, stride=BOX), :] = part[PAIRS:]
            return carry

        lax.fori_loop(0, HALF // 4, x_forward, 0)

    def y_steps(i, carry):
        parts = []
        for j in range(4):
            pair = step * 8 + i * 4 + j
            base = pl.multiple_of(pair * BOX, BOX)
            first = mid_ref[pl.ds(base, HALF), :]
            second = mid_ref[pl.ds(base + HALF, HALF), :]
            even, odd = exchange(first, second)
            parts.append(doubled(jnp.concatenate([even, odd], axis=0)))
        spatial = jnp.dot(forward_ref[...], jnp.concatenate(parts, axis=1), preferred_element_type=jnp.float32)
        parts = []
        for j in range(4):
            parts.append(doubled(spatial[:, j * 128 : (j + 1) * 128] * field_ref[i * 4 + j]))
        result = jnp.dot(backward_ref[...], jnp.concatenate(parts, axis=1), preferred_element_type=jnp.float32)
        for j in range(4):
            pair = step * 8 + i * 4 + j
            mid_ref[pl.ds(pl.multiple_of(pair * BOX, BOX), BOX), :] = result[:, j * 128 : (j + 1) * 128]
        return carry

    lax.fori_loop(0, 2, y_steps, 0)

    @pl.when(step == pl.num_programs(0) - 1)
    def _():
        def x_backward(i, carry):
            parts = []
            for j in range(4):
                k = i * 4 + j
                first = mid_ref[pl.ds(k, PAIRS, stride=BOX), :]
                second = mid_ref[pl.ds(k + HALF, PAIRS, stride=BOX), :]
                even, odd = exchange(first, second)
                parts.append(doubled(jnp.concatenate([even, odd], axis=0)))
            result = jnp.dot(backward_ref[...], jnp.concatenate(parts, axis=1), preferred_element_type=jnp.float32)
            for j in range(4):
                k = i * 4 + j
                part = result[:, j * 128 : (j + 1) * 128]
                grid_ref[pl.ds(pl.multiple_of(k * BOX, BOX), BOX), :] = jnp.where(low, part, pltpu.roll(part, 32, 1))
                grid_ref[pl.ds(pl.multiple_of((k + HALF) * BOX, BOX), BOX), :] = jnp.where(
                    low, pltpu.roll(part, 96, 1), part
                )
            return carry

        lax.fori_loop(0, HALF // 4, x_backward, 0)
        select_row = lax.broadcasted_iota(jnp.int32, (64, 128), 0)
        select_column = lax.broadcasted_iota(jnp.int32, (64, 128), 1)
        select = jnp.where(select_column == select_row // 32 * 64 + select_row % 32, 1.0, 0.0).astype(jnp.bfloat16)

        def group(p, carry):
            def pick(t, inner):
                base = pl.multiple_of(t * 128, 128)
                first = p * SLOTS + base
                for u in range(128):
                    stage_b[u : u + 1, :] = grid_ref[pl.ds(place_ref[first + u], 1), :]
                out_ref[p, :, pl.ds(base, 128)] = lax.dot_general(
                    select,
                    stage_b[...].astype(jnp.bfloat16),
                    (((1,), (1,)), ((), ())),
                    preferred_element_type=jnp.float32,
                ).astype(jnp.bfloat16)
                return inner

            lax.fori_loop(0, count_ref[p], pick, carry)

            def blank(t, inner):
                out_ref[p, :, pl.ds(pl.multiple_of(t * 128, 128), 128)] = jnp.zeros((64, 128), jnp.bfloat16)
                return inner

            return lax.fori_loop(count_ref[p], SLOTS // 128, blank, carry)

        lax.fori_loop(0, GROUPS, group, 0)


def plane_call(place, count, wire, field, forward, backward):
    whole = lambda shape: pl.BlockSpec(shape, lambda i: (0,) * len(shape), pipeline_mode=pl.Buffered(1))
    return pl.pallas_call(
        plane_kernel,
        grid=(PAIRS // 8,),
        in_specs=[
            pl.BlockSpec(memory_space=pltpu.SMEM),
            pl.BlockSpec(memory_space=pltpu.SMEM),
            whole((GROUPS, 64, SLOTS)),
            pl.BlockSpec((8, GRID, 128), lambda i: (i, 0, 0)),
            whole((GRID, 2 * BOX)),
            whole((BOX, 2 * GRID)),
        ],
        out_specs=whole((GROUPS, 64, SLOTS)),
        out_shape=jax.ShapeDtypeStruct((GROUPS, 64, SLOTS), jnp.bfloat16),
        scratch_shapes=[
            pltpu.VMEM((ROWS + 8, 128), jnp.float32),
            pltpu.VMEM((PAIRS * BOX, 128), jnp.float32),
            pltpu.VMEM((128, 128), jnp.float32),
            pltpu.VMEM((128, 128), jnp.float32),
        ],
        compiler_params=pltpu.CompilerParams(vmem_limit_bytes=56 * MIB),
        cost_estimate=pl.CostEstimate(flops=13_000_000_000, bytes_accessed=24_000_000, transcendentals=0),
        name="planes",
    )(place, count, wire, field, forward, backward)


def local(orbitals, potential, stick_column, column_slot):
    z_forward, z_backward, forward, backward = (jnp.asarray(table) for table in tables())
    live_all = stick_column >= 0
    own = lax.dynamic_slice_in_dim(stick_column, lax.axis_index("fft") * SLOTS, SLOTS)
    live = (own >= 0).astype(jnp.float32)[None, :]
    column_x, column_y = stick_column // GRID, stick_column % GRID
    box_x = jnp.where(column_x < GRID // 2, column_x + HALF, column_x - (GRID - HALF))
    box_y = jnp.where(column_y < GRID // 2, column_y + HALF, column_y - (GRID - HALF))
    place = jnp.where(live_all, box_y * BOX + box_x, ROWS)
    count = (jnp.sum(live_all.reshape(GROUPS, SLOTS).astype(jnp.int32), axis=1) + 127) // 128
    field = jnp.pad(potential.reshape(PLANES, 2, PAIRS, GRID), ((0, 1), (0, 0), (0, 0), (0, 0)))
    field = field.transpose(2, 3, 1, 0)[:, :, None, :, None, :]
    field = jnp.broadcast_to(field, (PAIRS, GRID, 2, 2, 2, ZPAD)).reshape(PAIRS, GRID, 128)

    wire, share = z_forward_call(orbitals.transpose(0, 2, 1), live, z_forward)
    wire = wire.reshape(GROUPS, 64, SLOTS)
    share = share.reshape(8, 128, SLOTS)
    incoming = lax.all_to_all(wire, "fft", split_axis=0, concat_axis=0, tiled=True)
    share = lax.all_to_all(share, "band", split_axis=0, concat_axis=0, tiled=True)
    share = share.reshape(8, 2, 2, 2, 16, SLOTS)
    product_s = gram_call(share, share, "gram_s")
    outgoing = plane_call(place, count, incoming, field, forward, backward)
    left = lax.all_to_all(incoming.reshape(8, 128, SLOTS), "band", split_axis=0, concat_axis=0, tiled=True)
    right = lax.all_to_all(outgoing.reshape(8, 128, SLOTS), "band", split_axis=0, concat_axis=0, tiled=True)
    returned = lax.all_to_all(outgoing, "fft", split_axis=0, concat_axis=0, tiled=True)
    product_h = gram_call(
        left.reshape(8, 2, 2, 2, 16, SLOTS), right.reshape(8, 2, 2, 2, 16, SLOTS), "gram_h"
    )
    applied = z_backward_call(returned.reshape(GROUPS, 2, 2, ZPAD, SLOTS), live, z_backward)
    products = lax.psum(jnp.concatenate([matrices(product_s), matrices(product_h)]), ("band", "fft"))
    products = products * (1.0 / (2.0 * STICKS * GRID))
    return (applied.transpose(0, 2, 1), products[0:2], products[2:4])


def solution(mesh):
    return jax.shard_map(
        local,
        mesh=mesh,
        in_specs=(P("band", "fft", None), P("fft", None), P(), P()),
        out_specs=(P("band", "fft", None), P(), P()),
        check_vma=False,
    )
```

```python
import functools
import math

import jax
import jax.numpy as jnp
import ml_dtypes
import numpy as np
from jax import lax
from jax.experimental import pallas as pl
from jax.experimental.pallas import tpu as pltpu
from jax.sharding import PartitionSpec as P

STICKS = 24576
GRID = 240
SLOTS = 1920
GROUPS = 16
PLANES = 15
ZPAD = 16
BOX = 192
HALF = BOX // 2
PAIRS = GRID // 2
ROWS = BOX * BOX
BLOCK = 384
PITCH = 200
PITCHB = 120
N1 = 8
N2 = 8
N4 = 8
MIB = 1 << 20


def trig():
    counter = np.arange(GRID, dtype=np.int32)
    phases = counter[:, None] * counter[None, :] % GRID
    angles = phases.astype(np.float32) * np.float32(2.0 * math.pi / GRID)
    factor = np.float32(1.0 / math.sqrt(GRID))
    cosine = (np.cos(angles) * factor).astype(ml_dtypes.bfloat16)
    sine = (np.sin(angles) * factor).astype(ml_dtypes.bfloat16)
    return cosine, sine


def tables():
    cosine, sine = trig()
    box = np.arange(BOX) - HALF
    box = np.where(box < 0, box + GRID, box)
    z_forward = np.zeros((GROUPS, 2, ZPAD, 2, GRID), ml_dtypes.bfloat16)
    cos_z = cosine.reshape(GROUPS, PLANES, GRID)
    sin_z = sine.reshape(GROUPS, PLANES, GRID)
    z_forward[:, 0, :PLANES, 0] = cos_z
    z_forward[:, 0, :PLANES, 1] = -sin_z
    z_forward[:, 1, :PLANES, 0] = sin_z
    z_forward[:, 1, :PLANES, 1] = cos_z
    z_forward = z_forward.reshape(GROUPS * 2 * ZPAD, 2 * GRID)
    z_backward = np.ascontiguousarray(z_forward.T)
    cos_box, sin_box = cosine[:, box], sine[:, box]
    forward = np.concatenate([cos_box, sin_box], axis=1)
    backward = np.concatenate([cos_box.T, -sin_box.T], axis=1)
    return z_forward, z_backward, forward, backward


def z_forward_kernel(orbit_ref, live_ref, table_ref, wire_ref, share_ref):
    masked = (orbit_ref[0].astype(jnp.float32) * live_ref[...]).astype(jnp.bfloat16)
    values = jnp.dot(table_ref[...], masked, preferred_element_type=jnp.float32).astype(jnp.bfloat16)
    lanes = values.shape[-1]
    wire_ref[...] = values.reshape(GROUPS, 2, 1, ZPAD, lanes)
    for c in range(2):
        for q in range(15):
            share_ref[q // 2, q % 2, c, 0] = masked[c * GRID + q * 16 : c * GRID + q * 16 + 16]
        share_ref[7, 1, c, 0] = jnp.zeros((16, lanes), jnp.bfloat16)


def z_forward_call(orbits, live, table):
    lanes = BLOCK
    return pl.pallas_call(
        z_forward_kernel,
        grid=(2, SLOTS // lanes),
        in_specs=[
            pl.BlockSpec((1, 2 * GRID, lanes), lambda b, t: (b, 0, t)),
            pl.BlockSpec((1, lanes), lambda b, t: (0, t)),
            pl.BlockSpec((512, 2 * GRID), lambda b, t: (0, 0)),
        ],
        out_specs=[
            pl.BlockSpec((GROUPS, 2, 1, ZPAD, lanes), lambda b, t: (0, 0, b, 0, t)),
            pl.BlockSpec((8, 2, 2, 1, 16, lanes), lambda b, t: (0, 0, 0, b, 0, t)),
        ],
        out_shape=[
            jax.ShapeDtypeStruct((GROUPS, 2, 2, ZPAD, SLOTS), jnp.bfloat16),
            jax.ShapeDtypeStruct((8, 4, 2, 2, 16, SLOTS), jnp.bfloat16),
        ],
        compiler_params=pltpu.CompilerParams(vmem_limit_bytes=60 * MIB),
        cost_estimate=pl.CostEstimate(flops=1_800_000_000, bytes_accessed=12_000_000, transcendentals=0),
        name="z_forward",
    )(orbits, live, table)


def z_backward_kernel(wire_ref, live_ref, table_ref, out_ref):
    lanes = wire_ref.shape[-1]
    values = wire_ref[...].reshape(512, lanes)
    applied = jnp.dot(table_ref[...], values, preferred_element_type=jnp.float32)
    out_ref[0] = (applied * live_ref[...]).astype(jnp.bfloat16)


def z_backward_call(wire, live, table):
    lanes = BLOCK
    return pl.pallas_call(
        z_backward_kernel,
        grid=(2, SLOTS // lanes),
        in_specs=[
            pl.BlockSpec((GROUPS, 2, 1, ZPAD, lanes), lambda b, t: (0, 0, b, 0, t)),
            pl.BlockSpec((1, lanes), lambda b, t: (0, t)),
            pl.BlockSpec((2 * GRID, 512), lambda b, t: (0, 0)),
        ],
        out_specs=pl.BlockSpec((1, 2 * GRID, lanes), lambda b, t: (b, 0, t)),
        out_shape=jax.ShapeDtypeStruct((2, 2 * GRID, SLOTS), jnp.bfloat16),
        compiler_params=pltpu.CompilerParams(vmem_limit_bytes=60 * MIB),
        cost_estimate=pl.CostEstimate(flops=1_800_000_000, bytes_accessed=8_000_000, transcendentals=0),
        name="z_backward",
    )(wire, live, table)


def gram_kernel(left_ref, *refs):
    *right_refs, out_ref, total = refs
    step = pl.program_id(0) * pl.num_programs(1) + pl.program_id(1)
    lanes = left_ref.shape[-1]
    left = left_ref[...].reshape(512, lanes)
    right = jnp.concatenate([ref[...].reshape(512 // len(right_refs), lanes) for ref in right_refs], axis=0)
    product = lax.dot_general(left, right, (((1,), (1,)), ((), ())), preferred_element_type=jnp.float32)

    @pl.when(step == 0)
    def _():
        total[...] = product

    @pl.when(step > 0)
    def _():
        total[...] += product

    @pl.when(step == pl.num_programs(0) * pl.num_programs(1) - 1)
    def _():
        row = lax.broadcasted_iota(jnp.int32, (512, 512), 0)
        column = lax.broadcasted_iota(jnp.int32, (512, 512), 1)
        diagonal = jnp.where(row % 16 == column % 16, total[...], 0.0)
        pick_row = lax.broadcasted_iota(jnp.int32, (32, 512), 0)
        pick_column = lax.broadcasted_iota(jnp.int32, (32, 512), 1)
        pick = jnp.where(pick_column // 16 == pick_row, 1.0, 0.0)
        by_row = jnp.dot(pick, diagonal, preferred_element_type=jnp.float32, precision=lax.Precision.HIGHEST)
        out_ref[...] = lax.dot_general(
            by_row,
            pick,
            (((1,), (1,)), ((), ())),
            preferred_element_type=jnp.float32,
            precision=lax.Precision.HIGHEST,
        )


def gram_call(left, rights, name):
    lanes = 640
    spec = pl.BlockSpec((8, 1, 2, 2, 16, lanes), lambda g, t: (0, g, 0, 0, 0, t))
    if len(rights) == 1:
        right_spec = spec
    else:
        right_spec = pl.BlockSpec((1, 2, 2, 16, lanes), lambda g, t: (g, 0, 0, 0, t))
    return pl.pallas_call(
        gram_kernel,
        grid=(2, SLOTS // lanes),
        in_specs=[spec] + [right_spec] * len(rights),
        out_specs=pl.BlockSpec((32, 32), lambda g, t: (0, 0)),
        out_shape=jax.ShapeDtypeStruct((32, 32), jnp.float32),
        scratch_shapes=[pltpu.VMEM((512, 512), jnp.float32)],
        compiler_params=pltpu.CompilerParams(vmem_limit_bytes=60 * MIB),
        cost_estimate=pl.CostEstimate(flops=2_000_000_000, bytes_accessed=8_000_000, transcendentals=0),
        name=name,
    )(left, *rights)


def matrices(product, order=None):
    parts = product.reshape(8, 2, 2, 8, 2, 2)
    if order is not None:
        parts = jnp.take(parts, order, axis=3)
    first = parts[:, 0, :, :, 0, :] + parts[:, 1, :, :, 1, :]
    second = parts[:, 0, :, :, 1, :] - parts[:, 1, :, :, 0, :]
    return jnp.stack([first.reshape(16, 16), second.reshape(16, 16)])


def summed(values, axis):
    size = lax.axis_size(axis)
    copies = jnp.broadcast_to(values[None], (size,) + values.shape)
    return jnp.sum(lax.all_to_all(copies, axis, split_axis=0, concat_axis=0, tiled=True), axis=0)


def spread_blocks(blocks, axis):
    size = lax.axis_size(axis)
    me = lax.axis_index(axis)
    result = []
    for shift in range(size):
        block = lax.dynamic_index_in_dim(blocks, (me + shift) % size, 0, keepdims=False)
        if shift:
            block = lax.ppermute(block, axis, [(i, (i + shift) % size) for i in range(size)])
        result.append(block)
    return result, (me - jnp.arange(size)) % size


def plane_kernel(
    place_ref, pick_ref, count_ref, upper_ref, wire_ref, field_ref, forward_ref, backward_ref, out_ref,
    grid_ref, mid_ref, stage_a, stage_b, list_ref
):
    step = pl.program_id(0)
    lane = lax.broadcasted_iota(jnp.int32, (1, 128), 1)
    low = lane % 64 < 32
    sign = jnp.where(lane < 64, -1.0, 1.0)

    def turned(values):
        return pltpu.roll(values, 64, 1) * sign

    def doubled(values):
        return jnp.concatenate([values, turned(values)], axis=0).astype(jnp.bfloat16)

    def exchange(first, second):
        return (
            jnp.where(low, first, pltpu.roll(second, 32, 1)),
            jnp.where(low, pltpu.roll(first, 96, 1), second),
        )

    @pl.when(step == 0)
    def _():
        def clear(i, carry):
            grid_ref[pl.ds(pl.multiple_of(i * 512, 512), 512), :] = jnp.zeros((512, 128), jnp.float32)
            return carry

        lax.fori_loop(0, ROWS // 512, clear, 0)

        def group(p, total):
            def note(t, inner):
                list_ref[inner] = p * 15 + t
                return inner + 1

            return lax.fori_loop(0, count_ref[p], note, total)

        total = lax.fori_loop(0, GROUPS, group, 0)
        list_ref[total] = list_ref[total - 1]
        list_ref[total + 1] = list_ref[total - 1]
        list_ref[total + 2] = list_ref[total - 1]
        list_ref[255] = (total + 1) // 2
        eye_row = lax.broadcasted_iota(jnp.int32, (128, 128), 0)
        eye_column = lax.broadcasted_iota(jnp.int32, (128, 128), 1)
        eye = jnp.where(eye_row == eye_column, 1.0, 0.0).astype(jnp.bfloat16)

        def rows_of(entry):
            p = entry // 15
            block = wire_ref[p, :, pl.ds(pl.multiple_of((entry - p * 15) * 128, 128), 128)]
            twice = jnp.concatenate([block[0:32], block[0:32], block[32:64], block[32:64]], axis=0)
            return lax.dot_general(eye, twice, (((1,), (1,)), ((), ())), preferred_element_type=jnp.float32)

        def spread(entry, stage):
            for u in range(128):
                grid_ref[pl.ds(place_ref[entry * 128 + u], 1), :] = stage[u : u + 1, :]

        def scatter(i, carry):
            entry = list_ref[2 * i]
            entry_b = list_ref[2 * i + 1]
            entry_c = list_ref[2 * i + 2]
            stage_b[...] = rows_of(entry_b)
            spread(entry, stage_a)
            stage_a[...] = rows_of(entry_c)
            spread(entry_b, stage_b)
            return carry

        stage_a[...] = rows_of(list_ref[0])
        lax.fori_loop(0, list_ref[255], scatter, 0)

        def x_forward(i, carry):
            parts = []
            for j in range(N1):
                k = i * N1 + j
                first = grid_ref[pl.ds(pl.multiple_of(k * BOX, BOX), BOX), :]
                second = grid_ref[pl.ds(pl.multiple_of((k + HALF) * BOX, BOX), BOX), :]
                parts.append(doubled(jnp.where(low, first, second)))
            result = jnp.dot(forward_ref[...], jnp.concatenate(parts, axis=1), preferred_element_type=jnp.float32)
            for j in range(N1):
                k = i * N1 + j
                part = result[:, j * 128 : (j + 1) * 128]
                mid_ref[pl.ds(k, PAIRS, stride=PITCH), :] = part[:PAIRS]
                mid_ref[pl.ds(k + HALF, PAIRS, stride=PITCH), :] = part[PAIRS:]
            return carry

        lax.fori_loop(0, HALF // N1, x_forward, 0)

    def y_steps(i, carry):
        parts = []
        for j in range(N2):
            pair = step * 8 + i * N2 + j
            base = pl.multiple_of(pair * PITCH, 8)
            first = mid_ref[pl.ds(base, HALF), :]
            second = mid_ref[pl.ds(base + HALF, HALF), :]
            even, odd = exchange(first, second)
            parts.append(doubled(jnp.concatenate([even, odd], axis=0)))
        spatial = jnp.dot(forward_ref[...], jnp.concatenate(parts, axis=1), preferred_element_type=jnp.float32)
        parts = []
        for j in range(N2):
            parts.append(doubled(spatial[:, j * 128 : (j + 1) * 128] * field_ref[i * N2 + j]))
        result = jnp.dot(backward_ref[...], jnp.concatenate(parts, axis=1), preferred_element_type=jnp.float32)
        for j in range(N2):
            pair = step * 8 + i * N2 + j
            grid_ref[pl.ds(pair, BOX, stride=PITCHB), :] = result[:, j * 128 : (j + 1) * 128]
        return carry

    lax.fori_loop(0, 8 // N2, y_steps, 0)

    @pl.when(step == pl.num_programs(0) - 1)
    def _():
        def x_backward(i, carry):
            parts = []
            for j in range(N4):
                k = i * N4 + j
                first = grid_ref[pl.ds(pl.multiple_of(k * PITCHB, 8), PAIRS), :]
                second = grid_ref[pl.ds(pl.multiple_of((k + HALF) * PITCHB, 8), PAIRS), :]
                even, odd = exchange(first, second)
                parts.append(doubled(jnp.concatenate([even, odd], axis=0)))
            result = jnp.dot(backward_ref[...], jnp.concatenate(parts, axis=1), preferred_element_type=jnp.float32)
            for j in range(N4):
                k = i * N4 + j
                mid_ref[pl.ds(pl.multiple_of(k * BOX, BOX), BOX), :] = result[:, j * 128 : (j + 1) * 128]
            return carry

        lax.fori_loop(0, HALF // N4, x_backward, 0)
        select_row = lax.broadcasted_iota(jnp.int32, (128, 128), 0)
        select_column = lax.broadcasted_iota(jnp.int32, (128, 128), 1)
        source = select_row % 64 // 32 * 64 + select_row // 64 * 32 + select_row % 32
        select = jnp.where(select_column == source, 1.0, 0.0).astype(jnp.bfloat16)
        origin = pl.multiple_of((step - (pl.num_programs(0) - 1)) * 8, 8)

        def gather(entry, stage):
            for u in range(128):
                stage[pl.ds(origin + u, 1), :] = mid_ref[pl.ds(pick_ref[entry * 128 + u], 1), :]

        def write(entry, stage):
            p = entry // 15
            base = pl.multiple_of((entry - p * 15) * 128, 128)
            both = lax.dot_general(
                select, stage[...].astype(jnp.bfloat16), (((1,), (1,)), ((), ())), preferred_element_type=jnp.float32
            )
            upper = upper_ref[pl.ds(entry, 1), :] > 0.0
            out_ref[p, :, pl.ds(base, 128)] = jnp.where(upper, both[64:], both[:64]).astype(jnp.bfloat16)

        def pick(i, carry):
            entry = list_ref[2 * i]
            entry_b = list_ref[2 * i + 1]
            entry_c = list_ref[2 * i + 2]
            gather(entry_b, stage_b)
            write(entry, stage_a)
            gather(entry_c, stage_a)
            write(entry_b, stage_b)
            return carry

        def group(p, carry):
            def blank(t, inner):
                out_ref[p, :, pl.ds(pl.multiple_of(t * 128, 128), 128)] = jnp.zeros((64, 128), jnp.bfloat16)
                return inner

            return lax.fori_loop(count_ref[p], SLOTS // 128, blank, carry)

        lax.fori_loop(0, GROUPS, group, 0)
        gather(list_ref[0], stage_a)
        lax.fori_loop(0, list_ref[255], pick, 0)


def plane_call(place, pick, count, upper, wire, field, forward, backward):
    whole = lambda shape: pl.BlockSpec(shape, lambda i: (0,) * len(shape), pipeline_mode=pl.Buffered(1))
    return pl.pallas_call(
        plane_kernel,
        grid=(PAIRS // 8,),
        in_specs=[
            pl.BlockSpec(memory_space=pltpu.SMEM),
            pl.BlockSpec(memory_space=pltpu.SMEM),
            pl.BlockSpec(memory_space=pltpu.SMEM),
            whole((GROUPS * SLOTS // 128, 128)),
            whole((GROUPS, 64, SLOTS)),
            pl.BlockSpec((8, GRID, 128), lambda i: (i, 0, 0)),
            whole((GRID, 2 * BOX)),
            whole((BOX, 2 * GRID)),
        ],
        out_specs=whole((GROUPS, 64, SLOTS)),
        out_shape=jax.ShapeDtypeStruct((GROUPS, 64, SLOTS), jnp.bfloat16),
        scratch_shapes=[
            pltpu.VMEM((ROWS + 8, 128), jnp.float32),
            pltpu.VMEM((PAIRS * PITCH, 128), jnp.float32),
            pltpu.VMEM((128, 128), jnp.float32),
            pltpu.VMEM((128, 128), jnp.float32),
            pltpu.SMEM((256,), jnp.int32),
        ],
        compiler_params=pltpu.CompilerParams(vmem_limit_bytes=56 * MIB),
        cost_estimate=pl.CostEstimate(flops=13_000_000_000, bytes_accessed=24_000_000, transcendentals=0),
        name="planes",
    )(place, pick, count, upper, wire, field, forward, backward)


def field_kernel(lower_ref, upper_ref, out_ref):
    blank = jnp.zeros((1, lower_ref.shape[-1]), jnp.float32)
    lower = jnp.concatenate([lower_ref[...], blank], axis=0)
    upper = jnp.concatenate([upper_ref[...], blank], axis=0)
    once = jnp.concatenate([lower, lower, upper, upper], axis=0)
    out_ref[...] = jnp.concatenate([once, once], axis=0).T.reshape(8, GRID, 128)


def field_call(potential):
    lanes = 8 * GRID
    return pl.pallas_call(
        field_kernel,
        grid=(PAIRS // 8,),
        in_specs=[
            pl.BlockSpec((PLANES, lanes), lambda i: (0, i)),
            pl.BlockSpec((PLANES, lanes), lambda i: (0, i + PAIRS // 8)),
        ],
        out_specs=pl.BlockSpec((8, GRID, 128), lambda i: (i, 0, 0)),
        out_shape=jax.ShapeDtypeStruct((PAIRS, GRID, 128), jnp.float32),
        compiler_params=pltpu.CompilerParams(vmem_limit_bytes=60 * MIB),
        cost_estimate=pl.CostEstimate(flops=0, bytes_accessed=18_000_000, transcendentals=0),
        name="field",
    )(potential, potential)


def local(orbitals, potential, stick_column, column_slot):
    z_forward, z_backward, forward, backward = (jnp.asarray(table) for table in tables())
    live_all = stick_column >= 0
    own = lax.dynamic_slice_in_dim(stick_column, lax.axis_index("fft") * SLOTS, SLOTS)
    live = (own >= 0).astype(jnp.float32)[None, :]
    column_x, column_y = stick_column // GRID, stick_column % GRID
    box_x = jnp.where(column_x < GRID // 2, column_x + HALF, column_x - (GRID - HALF))
    box_y = jnp.where(column_y < GRID // 2, column_y + HALF, column_y - (GRID - HALF))
    place = jnp.where(live_all, box_y * BOX + box_x, ROWS)
    count = (jnp.sum(live_all.reshape(GROUPS, SLOTS).astype(jnp.int32), axis=1) + 127) // 128
    upper = live_all & (box_y >= HALF)
    choose = jnp.where(live_all, jnp.where(upper, box_y - HALF, box_y) * BOX + box_x, 0)
    upper = upper.astype(jnp.float32).reshape(GROUPS * SLOTS // 128, 128)
    field = field_call(potential)

    wire, share = z_forward_call(orbitals.transpose(0, 2, 1), live, z_forward)
    share = share.reshape(8, 256, SLOTS)
    incoming = lax.all_to_all(wire.reshape(GROUPS, 64, SLOTS), "fft", split_axis=0, concat_axis=0, tiled=True)
    share, field, place, choose, count, upper = lax.optimization_barrier(
        (share, field, place, choose, count, upper)
    )
    shared = share.at[:, 128:].set(incoming.reshape(8, 128, SLOTS))
    shared = lax.all_to_all(shared, "band", split_axis=0, concat_axis=0, tiled=True)
    outgoing = plane_call(place, choose, count, upper, incoming, field, forward, backward)
    returned = lax.all_to_all(outgoing, "fft", split_axis=0, concat_axis=0, tiled=True)
    rights, order = spread_blocks(outgoing.reshape(8, 2, 2, 2, 16, SLOTS), "band")
    share = shared[:, :128].reshape(8, 2, 2, 2, 16, SLOTS)
    left = shared[:, 128:].reshape(8, 2, 2, 2, 16, SLOTS)
    product_s = gram_call(share, [share], "gram_s")
    product_h = gram_call(left, rights, "gram_h")
    product_s, product_h, returned = lax.optimization_barrier((product_s, product_h, returned))
    applied = z_backward_call(returned.reshape(GROUPS, 2, 2, ZPAD, SLOTS), live, z_backward)
    products = jnp.concatenate([matrices(product_s), matrices(product_h, order)])
    products = summed(summed(products, "fft"), "band") * (1.0 / (2.0 * STICKS * GRID))
    return (applied.transpose(0, 2, 1), products[0:2], products[2:4])


def solution(mesh):
    return jax.shard_map(
        local,
        mesh=mesh,
        in_specs=(P("band", "fft", None), P("fft", None), P(), P()),
        out_specs=(P("band", "fft", None), P(), P()),
        check_vma=False,
    )
```

```python
import functools
import math

import jax
import jax.numpy as jnp
import ml_dtypes
import numpy as np
from jax import lax
from jax.experimental import pallas as pl
from jax.experimental.pallas import tpu as pltpu
from jax.sharding import PartitionSpec as P

STICKS = 24576
GRID = 240
SLOTS = 1920
GROUPS = 16
PLANES = 15
ZPAD = 16
BOX = 192
HALF = BOX // 2
PAIRS = GRID // 2
ROWS = BOX * BOX
PITCH = 200
PITCHB = 120
PB = 24
N1 = 8
N2 = 12
N4 = 8
MIB = 1 << 20


def trig():
    counter = np.arange(GRID, dtype=np.int32)
    phases = counter[:, None] * counter[None, :] % GRID
    angles = phases.astype(np.float32) * np.float32(2.0 * math.pi / GRID)
    factor = np.float32(1.0 / math.sqrt(GRID))
    cosine = (np.cos(angles) * factor).astype(ml_dtypes.bfloat16)
    sine = (np.sin(angles) * factor).astype(ml_dtypes.bfloat16)
    return cosine, sine


def tables():
    cosine, sine = trig()
    box = np.arange(BOX) - HALF
    box = np.where(box < 0, box + GRID, box)
    z_forward = np.zeros((GROUPS, 2, ZPAD, 2, GRID), ml_dtypes.bfloat16)
    cos_z = cosine.reshape(GROUPS, PLANES, GRID)
    sin_z = sine.reshape(GROUPS, PLANES, GRID)
    z_forward[:, 0, :PLANES, 0] = cos_z
    z_forward[:, 0, :PLANES, 1] = -sin_z
    z_forward[:, 1, :PLANES, 0] = sin_z
    z_forward[:, 1, :PLANES, 1] = cos_z
    z_forward = z_forward.reshape(GROUPS * 2 * ZPAD, 2 * GRID)
    z_backward = np.ascontiguousarray(z_forward.T)
    cos_box, sin_box = cosine[:, box], sine[:, box]
    forward = np.concatenate([cos_box, sin_box], axis=1)
    backward = np.concatenate([cos_box.T, -sin_box.T], axis=1)
    return z_forward, z_backward, forward, backward


def z_forward_kernel(orbit_ref, live_ref, table_ref, wire_ref, share_ref, masked_ref):
    masked_ref[...] = (orbit_ref[0].astype(jnp.float32) * live_ref[...]).astype(jnp.bfloat16)
    for c in range(2):
        for q in range(15):
            start = c * GRID + q * 16
            share_ref[q // 2, q % 2, c, 0] = masked_ref[start : start + 16]
        share_ref[7, 1, c, 0] = jnp.zeros((16, SLOTS), jnp.bfloat16)
    values = jnp.dot(table_ref[...], masked_ref[...], preferred_element_type=jnp.float32).astype(jnp.bfloat16)
    wire_ref[...] = values.reshape(GROUPS, 2, 1, ZPAD, SLOTS)


def z_forward_call(orbits, live, table):
    return pl.pallas_call(
        z_forward_kernel,
        grid=(2,),
        in_specs=[
            pl.BlockSpec((1, 2 * GRID, SLOTS), lambda b: (b, 0, 0)),
            pl.BlockSpec((1, SLOTS), lambda b: (0, 0)),
            pl.BlockSpec((512, 2 * GRID), lambda b: (0, 0)),
        ],
        out_specs=[
            pl.BlockSpec((GROUPS, 2, 1, ZPAD, SLOTS), lambda b: (0, 0, b, 0, 0)),
            pl.BlockSpec((8, 2, 2, 1, 16, SLOTS), lambda b: (0, 0, 0, b, 0, 0)),
        ],
        out_shape=[
            jax.ShapeDtypeStruct((GROUPS, 2, 2, ZPAD, SLOTS), jnp.bfloat16),
            jax.ShapeDtypeStruct((8, 2, 2, 2, 16, SLOTS), jnp.bfloat16),
        ],
        scratch_shapes=[pltpu.VMEM((2 * GRID, SLOTS), jnp.bfloat16)],
        compiler_params=pltpu.CompilerParams(vmem_limit_bytes=60 * MIB),
        cost_estimate=pl.CostEstimate(flops=1_800_000_000, bytes_accessed=12_000_000, transcendentals=0),
        name="z_forward",
    )(orbits, live, table)


def z_backward_kernel(wire_ref, live_ref, table_ref, out_ref):
    values = wire_ref[...].reshape(512, SLOTS)
    applied = jnp.dot(table_ref[...], values, preferred_element_type=jnp.float32)
    out_ref[0] = (applied * live_ref[...]).astype(jnp.bfloat16)


def z_backward_call(wire, live, table):
    return pl.pallas_call(
        z_backward_kernel,
        grid=(2,),
        in_specs=[
            pl.BlockSpec((GROUPS, 2, 1, ZPAD, SLOTS), lambda b: (0, 0, b, 0, 0)),
            pl.BlockSpec((1, SLOTS), lambda b: (0, 0)),
            pl.BlockSpec((2 * GRID, 512), lambda b: (0, 0)),
        ],
        out_specs=pl.BlockSpec((1, 2 * GRID, SLOTS), lambda b: (b, 0, 0)),
        out_shape=jax.ShapeDtypeStruct((2, 2 * GRID, SLOTS), jnp.bfloat16),
        compiler_params=pltpu.CompilerParams(vmem_limit_bytes=60 * MIB),
        cost_estimate=pl.CostEstimate(flops=1_800_000_000, bytes_accessed=8_000_000, transcendentals=0),
        name="z_backward",
    )(wire, live, table)


def gram_kernel(me_ref, *refs, left_blocks, right_blocks, first_lane):
    left_refs, right_refs = refs[:left_blocks], refs[left_blocks : left_blocks + right_blocks]
    out_ref, total = refs[left_blocks + right_blocks :]
    step = pl.program_id(0)
    left = jnp.concatenate([ref[...].reshape(-1, SLOTS) for ref in left_refs], axis=0)
    if right_blocks:
        right = jnp.concatenate([ref[...].reshape(-1, SLOTS) for ref in right_refs], axis=0)
    else:
        right = left
    product = lax.dot_general(left, right, (((1,), (1,)), ((), ())), preferred_element_type=jnp.float32)

    @pl.when(step == 0)
    def _():
        total[...] = product

    def band_of(index, rotated):
        source = index // 64
        if rotated:
            chip, core = me_ref[0] // 2, me_ref[0] % 2
            source = (chip + 4 - source // 2) % 4 * 2 + (core + source) % 2
        return source * 2 + index // 16 % 2

    @pl.when(step == 1)
    def _():
        row = lax.broadcasted_iota(jnp.int32, (512, 512), 0)
        column = lax.broadcasted_iota(jnp.int32, (512, 512), 1)
        diagonal = jnp.where(row % 16 == column % 16, total[...] + product, 0.0)
        band = lax.broadcasted_iota(jnp.int32, (32, 512), 0)
        index = lax.broadcasted_iota(jnp.int32, (32, 512), 1)
        pick = (band % 16 == band_of(index, left_blocks > 1)) & (band // 16 == index // 32 % 2)
        by_band = jnp.dot(
            jnp.where(pick, 1.0, 0.0), diagonal, preferred_element_type=jnp.float32, precision=lax.Precision.HIGHEST
        )
        lane = lax.broadcasted_iota(jnp.int32, (128, 512), 0) - first_lane
        index = lax.broadcasted_iota(jnp.int32, (128, 512), 1)
        match = (lane >= 0) & (lane < 32) & (lane % 16 == band_of(index, right_blocks != 1))
        part = index // 32 % 2
        second = lane // 16 == 1
        with_real = jnp.where(match & (part == jnp.where(second, 1, 0)), 1.0, 0.0)
        with_imag = jnp.where(match & (part == jnp.where(second, 0, 1)), jnp.where(second, -1.0, 1.0), 0.0)
        dims = (((1,), (1,)), ((), ()))
        out_ref[...] = lax.dot_general(
            by_band[:16], with_real, dims, preferred_element_type=jnp.float32, precision=lax.Precision.HIGHEST
        ) + lax.dot_general(
            by_band[16:], with_imag, dims, preferred_element_type=jnp.float32, precision=lax.Precision.HIGHEST
        )


def gram_call(me, lefts, rights, first_lane, name):
    whole = pl.BlockSpec((8, 1, 2, 2, 16, SLOTS), lambda g: (0, g, 0, 0, 0, 0))
    piece = pl.BlockSpec((2, 1, 2, 2, 16, SLOTS), lambda g: (0, g, 0, 0, 0, 0))
    specs = [whole if len(lefts) == 1 else piece] * len(lefts) + [whole if len(rights) == 1 else piece] * len(rights)
    return pl.pallas_call(
        functools.partial(
            gram_kernel, left_blocks=len(lefts), right_blocks=len(rights), first_lane=first_lane
        ),
        grid=(2,),
        in_specs=[pl.BlockSpec(memory_space=pltpu.SMEM)] + specs,
        out_specs=pl.BlockSpec((16, 128), lambda g: (0, 0)),
        out_shape=jax.ShapeDtypeStruct((16, 128), jnp.float32),
        scratch_shapes=[pltpu.VMEM((512, 512), jnp.float32)],
        compiler_params=pltpu.CompilerParams(vmem_limit_bytes=60 * MIB),
        cost_estimate=pl.CostEstimate(flops=2_000_000_000, bytes_accessed=8_000_000, transcendentals=0),
        name=name,
    )(me, *lefts, *rights)


def summed(values, axis):
    size = lax.axis_size(axis)
    copies = jnp.broadcast_to(values[None], (size,) + values.shape)
    return jnp.sum(lax.all_to_all(copies, axis, split_axis=0, concat_axis=0, tiled=True), axis=0)


def spread_blocks(blocks, axis):
    me = lax.axis_index(axis)
    chip, core = me // 2, me % 2
    halves = blocks.reshape((4, 2) + blocks.shape[1:])
    kept = lax.dynamic_index_in_dim(halves, core, 1, keepdims=False)
    given = lax.dynamic_index_in_dim(halves, 1 - core, 1, keepdims=False)
    got = lax.ppermute(given, axis, [(i, i ^ 1) for i in range(8)])
    result = []
    for shift in range(4):
        target = (chip + shift) % 4
        pair = jnp.concatenate(
            [lax.dynamic_slice_in_dim(kept, target, 1, 0), lax.dynamic_slice_in_dim(got, target, 1, 0)], axis=0
        )
        if shift:
            pair = lax.ppermute(pair, axis, [(i, (i // 2 + shift) % 4 * 2 + i % 2) for i in range(8)])
        result.append(pair)
    return result


def plane_kernel(
    place_ref, count_ref, upper_ref, wire_ref, field_ref, forward_ref, backward_ref, out_ref,
    grid_ref, mid_ref, back_ref, stage_a, stage_b, list_ref
):
    step = pl.program_id(0)
    lane = lax.broadcasted_iota(jnp.int32, (1, 128), 1)
    low = lane % 64 < 32
    sign = jnp.where(lane < 64, -1.0, 1.0).astype(jnp.bfloat16)

    def doubled(values):
        values = values.astype(jnp.bfloat16)
        return jnp.concatenate([values, pltpu.roll(values, 64, 1) * sign], axis=0)

    def exchange(first, second):
        return (
            jnp.where(low, first, pltpu.roll(second, 32, 1)),
            jnp.where(low, pltpu.roll(first, 96, 1), second),
        )

    @pl.when(step == 0)
    def _():
        def clear(i, carry):
            grid_ref[pl.ds(pl.multiple_of(i * 512, 512), 512), :] = jnp.zeros((512, 128), jnp.float32)
            return carry

        lax.fori_loop(0, ROWS // 512, clear, 0)
        grid_ref[pl.ds(ROWS, 8), :] = jnp.zeros((8, 128), jnp.float32)

        def group(p, total):
            def note(t, inner):
                list_ref[inner] = p * 15 + t
                return inner + 1

            return lax.fori_loop(0, count_ref[p], note, total)

        total = lax.fori_loop(0, GROUPS, group, 0)
        list_ref[total] = list_ref[total - 1]
        list_ref[total + 1] = list_ref[total - 1]
        list_ref[total + 2] = list_ref[total - 1]
        list_ref[255] = (total + 1) // 2
        eye_row = lax.broadcasted_iota(jnp.int32, (128, 128), 0)
        eye_column = lax.broadcasted_iota(jnp.int32, (128, 128), 1)
        eye = jnp.where(eye_row == eye_column, 1.0, 0.0).astype(jnp.bfloat16)

        def rows_of(entry):
            p = entry // 15
            block = wire_ref[p, :, pl.ds(pl.multiple_of((entry - p * 15) * 128, 128), 128)]
            twice = jnp.concatenate([block[0:32], block[0:32], block[32:64], block[32:64]], axis=0)
            return lax.dot_general(eye, twice, (((1,), (1,)), ((), ())), preferred_element_type=jnp.float32)

        def spread(entry, stage):
            for u in range(128):
                grid_ref[pl.ds(place_ref[entry * 128 + u], 1), :] = stage[u : u + 1, :]

        def scatter(i, carry):
            entry = list_ref[2 * i]
            entry_b = list_ref[2 * i + 1]
            entry_c = list_ref[2 * i + 2]
            stage_b[...] = rows_of(entry_b)
            spread(entry, stage_a)
            stage_a[...] = rows_of(entry_c)
            spread(entry_b, stage_b)
            return carry

        stage_a[...] = rows_of(list_ref[0])
        lax.fori_loop(0, list_ref[255], scatter, 0)

        def x_forward(i, carry):
            parts = []
            for j in range(N1):
                k = i * N1 + j
                first = grid_ref[pl.ds(pl.multiple_of(k * BOX, BOX), BOX), :]
                second = grid_ref[pl.ds(pl.multiple_of((k + HALF) * BOX, BOX), BOX), :]
                parts.append(doubled(jnp.where(low, first, second)))
            result = jnp.dot(forward_ref[...], jnp.concatenate(parts, axis=1), preferred_element_type=jnp.float32)
            for j in range(N1):
                k = i * N1 + j
                part = result[:, j * 128 : (j + 1) * 128]
                mid_ref[pl.ds(k, PAIRS, stride=PITCH), :] = part[:PAIRS]
                mid_ref[pl.ds(k + HALF, PAIRS, stride=PITCH), :] = part[PAIRS:]
            return carry

        lax.fori_loop(0, HALF // N1, x_forward, 0)

    def y_steps(i, carry):
        parts = []
        for j in range(N2):
            pair = step * PB + i * N2 + j
            base = pl.multiple_of(pair * PITCH, 8)
            first = mid_ref[pl.ds(base, HALF), :]
            second = mid_ref[pl.ds(base + HALF, HALF), :]
            even, odd = exchange(first, second)
            parts.append(doubled(jnp.concatenate([even, odd], axis=0)))
        spatial = jnp.dot(forward_ref[...], jnp.concatenate(parts, axis=1), preferred_element_type=jnp.float32)
        parts = []
        for j in range(N2):
            parts.append(doubled(spatial[:, j * 128 : (j + 1) * 128] * field_ref[i * N2 + j]))
        result = jnp.dot(backward_ref[...], jnp.concatenate(parts, axis=1), preferred_element_type=jnp.float32)
        for j in range(N2):
            pair = step * PB + i * N2 + j
            back_ref[pl.ds(pair, BOX, stride=PITCHB), :] = result[:, j * 128 : (j + 1) * 128]
        return carry

    lax.fori_loop(0, PB // N2, y_steps, 0)

    @pl.when(step == pl.num_programs(0) - 1)
    def _():
        def x_backward(i, carry):
            parts = []
            for j in range(N4):
                k = i * N4 + j
                first = back_ref[pl.ds(pl.multiple_of(k * PITCHB, 8), PAIRS), :]
                second = back_ref[pl.ds(pl.multiple_of((k + HALF) * PITCHB, 8), PAIRS), :]
                even, odd = exchange(first, second)
                parts.append(doubled(jnp.concatenate([even, odd], axis=0)))
            result = jnp.dot(backward_ref[...], jnp.concatenate(parts, axis=1), preferred_element_type=jnp.float32)
            for j in range(N4):
                k = i * N4 + j
                part = result[:, j * 128 : (j + 1) * 128]
                grid_ref[pl.ds(pl.multiple_of(k * BOX, BOX), BOX), :] = part
                grid_ref[pl.ds(pl.multiple_of((k + HALF) * BOX, BOX), BOX), :] = part
            return carry

        lax.fori_loop(0, HALF // N4, x_backward, 0)
        select_row = lax.broadcasted_iota(jnp.int32, (128, 128), 0)
        select_column = lax.broadcasted_iota(jnp.int32, (128, 128), 1)
        source = select_row % 64 // 32 * 64 + select_row // 64 * 32 + select_row % 32
        select = jnp.where(select_column == source, 1.0, 0.0).astype(jnp.bfloat16)
        origin = pl.multiple_of((step - (pl.num_programs(0) - 1)) * 8, 8)

        def gather(entry, stage):
            for u in range(128):
                stage[pl.ds(origin + u, 1), :] = grid_ref[pl.ds(place_ref[entry * 128 + u], 1), :]

        def write(entry, stage):
            p = entry // 15
            base = pl.multiple_of((entry - p * 15) * 128, 128)
            both = lax.dot_general(
                select, stage[...].astype(jnp.bfloat16), (((1,), (1,)), ((), ())), preferred_element_type=jnp.float32
            )
            upper = upper_ref[pl.ds(entry, 1), :] > 0.0
            out_ref[p, :, pl.ds(base, 128)] = jnp.where(upper, both[64:], both[:64]).astype(jnp.bfloat16)

        def pick(i, carry):
            entry = list_ref[2 * i]
            entry_b = list_ref[2 * i + 1]
            entry_c = list_ref[2 * i + 2]
            gather(entry_b, stage_b)
            write(entry, stage_a)
            gather(entry_c, stage_a)
            write(entry_b, stage_b)
            return carry

        def group(p, carry):
            def blank(t, inner):
                out_ref[p, :, pl.ds(pl.multiple_of(t * 128, 128), 128)] = jnp.zeros((64, 128), jnp.bfloat16)
                return inner

            return lax.fori_loop(count_ref[p], SLOTS // 128, blank, carry)

        lax.fori_loop(0, GROUPS, group, 0)
        gather(list_ref[0], stage_a)
        lax.fori_loop(0, list_ref[255], pick, 0)


def plane_call(place, count, upper, wire, field, forward, backward):
    whole = lambda shape: pl.BlockSpec(shape, lambda i: (0,) * len(shape), pipeline_mode=pl.Buffered(1))
    return pl.pallas_call(
        plane_kernel,
        grid=(PAIRS // PB,),
        in_specs=[
            pl.BlockSpec(memory_space=pltpu.SMEM),
            pl.BlockSpec(memory_space=pltpu.SMEM),
            whole((GROUPS * SLOTS // 128, 128)),
            whole((GROUPS, 64, SLOTS)),
            pl.BlockSpec((PB, GRID, 128), lambda i: (i, 0, 0)),
            whole((GRID, 2 * BOX)),
            whole((BOX, 2 * GRID)),
        ],
        out_specs=whole((GROUPS, 64, SLOTS)),
        out_shape=jax.ShapeDtypeStruct((GROUPS, 64, SLOTS), jnp.bfloat16),
        scratch_shapes=[
            pltpu.VMEM((ROWS + 8, 128), jnp.float32),
            pltpu.VMEM((PAIRS * PITCH, 128), jnp.float32),
            pltpu.VMEM((BOX * PITCHB, 128), jnp.float32),
            pltpu.VMEM((128, 128), jnp.float32),
            pltpu.VMEM((128, 128), jnp.float32),
            pltpu.SMEM((256,), jnp.int32),
        ],
        compiler_params=pltpu.CompilerParams(vmem_limit_bytes=62 * MIB),
        cost_estimate=pl.CostEstimate(flops=13_000_000_000, bytes_accessed=24_000_000, transcendentals=0),
        name="planes",
    )(place, count, upper, wire, field, forward, backward)


def field_kernel(lower_ref, upper_ref, out_ref):
    blank = jnp.zeros((1, lower_ref.shape[-1]), jnp.float32)
    lower = jnp.concatenate([lower_ref[...], blank], axis=0)
    upper = jnp.concatenate([upper_ref[...], blank], axis=0)
    once = jnp.concatenate([lower, lower, upper, upper], axis=0)
    out_ref[...] = jnp.concatenate([once, once], axis=0).T.reshape(8, GRID, 128)


def field_call(potential):
    lanes = 8 * GRID
    return pl.pallas_call(
        field_kernel,
        grid=(PAIRS // 8,),
        in_specs=[
            pl.BlockSpec((PLANES, lanes), lambda i: (0, i)),
            pl.BlockSpec((PLANES, lanes), lambda i: (0, i + PAIRS // 8)),
        ],
        out_specs=pl.BlockSpec((8, GRID, 128), lambda i: (i, 0, 0)),
        out_shape=jax.ShapeDtypeStruct((PAIRS, GRID, 128), jnp.float32),
        compiler_params=pltpu.CompilerParams(vmem_limit_bytes=60 * MIB),
        cost_estimate=pl.CostEstimate(flops=0, bytes_accessed=18_000_000, transcendentals=0),
        name="field",
    )(potential, potential)


def local(orbitals, potential, stick_column, column_slot):
    z_forward, z_backward, forward, backward = (jnp.asarray(table) for table in tables())
    live_all = stick_column >= 0
    own = lax.dynamic_slice_in_dim(stick_column, lax.axis_index("fft") * SLOTS, SLOTS)
    live = (own >= 0).astype(jnp.float32)[None, :]
    column_x, column_y = stick_column // GRID, stick_column % GRID
    box_x = jnp.where(column_x < GRID // 2, column_x + HALF, column_x - (GRID - HALF))
    box_y = jnp.where(column_y < GRID // 2, column_y + HALF, column_y - (GRID - HALF))
    place = jnp.where(live_all, box_y * BOX + box_x, ROWS)
    count = (jnp.sum(live_all.reshape(GROUPS, SLOTS).astype(jnp.int32), axis=1) + 127) // 128
    upper = (live_all & (box_y >= HALF)).astype(jnp.float32).reshape(GROUPS * SLOTS // 128, 128)
    me = lax.axis_index("band").astype(jnp.int32)[None]
    field = field_call(potential)

    wire, share = z_forward_call(orbitals.transpose(0, 2, 1), live, z_forward)
    incoming = lax.all_to_all(wire.reshape(GROUPS, 64, SLOTS), "fft", split_axis=0, concat_axis=0, tiled=True)
    shares = spread_blocks(share, "band")
    incoming, field, place, count, upper, *shares = lax.optimization_barrier(
        (incoming, field, place, count, upper, *shares)
    )
    left = lax.all_to_all(incoming.reshape(8, 128, SLOTS), "band", split_axis=0, concat_axis=0, tiled=True)
    outgoing = plane_call(place, count, upper, incoming, field, forward, backward)
    returned = lax.all_to_all(outgoing, "fft", split_axis=0, concat_axis=0, tiled=True)
    rights = spread_blocks(outgoing.reshape(8, 2, 2, 2, 16, SLOTS), "band")
    product_h = gram_call(me, [left.reshape(8, 2, 2, 2, 16, SLOTS)], rights, 32, "gram_h")
    product_s = gram_call(me, shares, [], 0, "gram_s")
    product_h, product_s, returned = lax.optimization_barrier((product_h, product_s, returned))
    products = product_s + product_h
    applied = z_backward_call(returned.reshape(GROUPS, 2, 2, ZPAD, SLOTS), live, z_backward)
    products = summed(summed(products, "band"), "fft") * (1.0 / (2.0 * STICKS * GRID))
    products = products[:, :64].reshape(16, 4, 16).transpose(1, 0, 2)
    return (applied.transpose(0, 2, 1), products[0:2], products[2:4])


def solution(mesh):
    return jax.shard_map(
        local,
        mesh=mesh,
        in_specs=(P("band", "fft", None), P("fft", None), P(), P()),
        out_specs=(P("band", "fft", None), P(), P()),
        check_vma=False,
    )
```

```python
import functools
import math

import jax
import jax.numpy as jnp
import ml_dtypes
import numpy as np
from jax import lax
from jax.experimental import pallas as pl
from jax.experimental.pallas import tpu as pltpu
from jax.sharding import PartitionSpec as P

STICKS = 24576
GRID = 240
SLOTS = 1920
GROUPS = 16
PLANES = 15
ZPAD = 16
BOX = 192
HALF = BOX // 2
PAIRS = GRID // 2
ROWS = BOX * BOX
PITCH = 200
PITCHB = 120
PB = 24
N1 = 8
N2 = 12
N4 = 8
MIB = 1 << 20


def trig():
    counter = np.arange(GRID, dtype=np.int32)
    phases = counter[:, None] * counter[None, :] % GRID
    angles = phases.astype(np.float32) * np.float32(2.0 * math.pi / GRID)
    factor = np.float32(1.0 / math.sqrt(GRID))
    cosine = (np.cos(angles) * factor).astype(ml_dtypes.bfloat16)
    sine = (np.sin(angles) * factor).astype(ml_dtypes.bfloat16)
    return cosine, sine


def tables():
    cosine, sine = trig()
    box = np.arange(BOX) - HALF
    box = np.where(box < 0, box + GRID, box)
    z_forward = np.zeros((GROUPS, 2, ZPAD, 2, GRID), ml_dtypes.bfloat16)
    cos_z = cosine.reshape(GROUPS, PLANES, GRID)
    sin_z = sine.reshape(GROUPS, PLANES, GRID)
    z_forward[:, 0, :PLANES, 0] = cos_z
    z_forward[:, 0, :PLANES, 1] = -sin_z
    z_forward[:, 1, :PLANES, 0] = sin_z
    z_forward[:, 1, :PLANES, 1] = cos_z
    z_forward = z_forward.reshape(GROUPS * 2 * ZPAD, 2 * GRID)
    z_backward = np.ascontiguousarray(z_forward.T)
    cos_box, sin_box = cosine[:, box], sine[:, box]
    forward = np.concatenate([cos_box, sin_box], axis=1)
    backward = np.concatenate([cos_box.T, -sin_box.T], axis=1)
    return z_forward, z_backward, forward, backward


def z_forward_kernel(core_ref, orbit_ref, live_ref, table_ref, wire_ref, kept_ref, given_ref, masked_ref):
    masked_ref[...] = (orbit_ref[0].astype(jnp.float32) * live_ref[...]).astype(jnp.bfloat16)
    for core in range(2):

        @pl.when(core_ref[0] == core)
        def _():
            for q in range(15):
                target = kept_ref if q // 2 % 2 == core else given_ref
                for c in range(2):
                    start = c * GRID + q * 16
                    target[q // 4, q % 2, c, 0] = masked_ref[start : start + 16]
            target = kept_ref if core == 1 else given_ref
            for c in range(2):
                target[3, 1, c, 0] = jnp.zeros((16, SLOTS), jnp.bfloat16)

    values = jnp.dot(table_ref[...], masked_ref[...], preferred_element_type=jnp.float32).astype(jnp.bfloat16)
    wire_ref[...] = values.reshape(GROUPS, 2, 1, ZPAD, SLOTS)


def z_forward_call(core, orbits, live, table):
    share = pl.BlockSpec((4, 2, 2, 1, 16, SLOTS), lambda b: (0, 0, 0, b, 0, 0))
    return pl.pallas_call(
        z_forward_kernel,
        grid=(2,),
        in_specs=[
            pl.BlockSpec(memory_space=pltpu.SMEM),
            pl.BlockSpec((1, 2 * GRID, SLOTS), lambda b: (b, 0, 0)),
            pl.BlockSpec((1, SLOTS), lambda b: (0, 0)),
            pl.BlockSpec((512, 2 * GRID), lambda b: (0, 0)),
        ],
        out_specs=[pl.BlockSpec((GROUPS, 2, 1, ZPAD, SLOTS), lambda b: (0, 0, b, 0, 0)), share, share],
        out_shape=[jax.ShapeDtypeStruct((GROUPS, 2, 2, ZPAD, SLOTS), jnp.bfloat16)]
        + [jax.ShapeDtypeStruct((4, 2, 2, 2, 16, SLOTS), jnp.bfloat16)] * 2,
        scratch_shapes=[pltpu.VMEM((2 * GRID, SLOTS), jnp.bfloat16)],
        compiler_params=pltpu.CompilerParams(vmem_limit_bytes=60 * MIB),
        cost_estimate=pl.CostEstimate(flops=1_800_000_000, bytes_accessed=12_000_000, transcendentals=0),
        name="z_forward",
    )(core, orbits, live, table)


def z_backward_kernel(wire_ref, live_ref, table_ref, out_ref):
    values = wire_ref[...].reshape(512, SLOTS)
    applied = jnp.dot(table_ref[...], values, preferred_element_type=jnp.float32)
    out_ref[0] = (applied * live_ref[...]).astype(jnp.bfloat16)


def z_backward_call(wire, live, table):
    return pl.pallas_call(
        z_backward_kernel,
        grid=(2,),
        in_specs=[
            pl.BlockSpec((GROUPS, 2, 1, ZPAD, SLOTS), lambda b: (0, 0, b, 0, 0)),
            pl.BlockSpec((1, SLOTS), lambda b: (0, 0)),
            pl.BlockSpec((2 * GRID, 512), lambda b: (0, 0)),
        ],
        out_specs=pl.BlockSpec((1, 2 * GRID, SLOTS), lambda b: (b, 0, 0)),
        out_shape=jax.ShapeDtypeStruct((2, 2 * GRID, SLOTS), jnp.bfloat16),
        compiler_params=pltpu.CompilerParams(vmem_limit_bytes=60 * MIB),
        cost_estimate=pl.CostEstimate(flops=1_800_000_000, bytes_accessed=8_000_000, transcendentals=0),
        name="z_backward",
    )(wire, live, table)


def side_by_side(refs):
    return jnp.concatenate([ref[...].reshape(-1, SLOTS) for ref in refs], axis=0)


def products_of(left, right):
    return lax.dot_general(left, right, (((1,), (1,)), ((), ())), preferred_element_type=jnp.float32)


def exact(left, right, transposed):
    dims = (((1,), (1 if transposed else 0,)), ((), ()))
    return lax.dot_general(left, right, dims, preferred_element_type=jnp.float32, precision=lax.Precision.HIGHEST)


def selector(me_ref, size, shifts):
    row = lax.broadcasted_iota(jnp.int32, (32, size), 0)
    index = lax.broadcasted_iota(jnp.int32, (32, size), 1)
    source = index // 64
    if shifts is not None:
        shift = source // 2
        for position, value in enumerate(shifts):
            shift = jnp.where(source // 2 == position, value, shift)
        source = (me_ref[0] // 2 + 4 - shift) % 4 * 2 + (me_ref[0] + source) % 2
    band = source * 2 + index // 16 % 2
    return jnp.where((row % 16 == band) & (row // 16 == index // 32 % 2), 1.0, 0.0)


def matched(total):
    row = lax.broadcasted_iota(jnp.int32, total.shape, 0)
    column = lax.broadcasted_iota(jnp.int32, total.shape, 1)
    return jnp.where(row % 16 == column % 16, total, 0.0)


def complex_lanes(table, first_lane):
    row = lax.broadcasted_iota(jnp.int32, (32, 128), 0)
    lane = lax.broadcasted_iota(jnp.int32, (32, 128), 1) - first_lane
    match = (lane >= 0) & (lane < 32) & (lane % 16 == row % 16)
    second, imag = lane // 16 == 1, row // 16 == 1
    with_real = jnp.where(match & (second == imag), 1.0, 0.0)
    with_imag = jnp.where(match & (second != imag), jnp.where(second, -1.0, 1.0), 0.0)
    return exact(table[:16], with_real, False) + exact(table[16:], with_imag, False)


def overlap_kernel(me_ref, *refs):
    *piece_refs, out_ref, total = refs
    step = pl.program_id(0)
    values = side_by_side(piece_refs)
    product = products_of(values, values)

    @pl.when(step == 0)
    def _():
        total[...] = product

    @pl.when(step == 1)
    def _():
        pick = selector(me_ref, 512, (0, 1, 2, 3))
        table = exact(exact(pick, matched(total[...] + product), False), pick, True)
        out_ref[...] = complex_lanes(table, 0)


def hamiltonian_kernel(me_ref, left_ref, left_far_ref, near_ref, before_ref, after_ref, far_ref, out_ref, *totals):
    total, total_far = totals
    step = pl.program_id(0)
    product = products_of(left_ref[...].reshape(512, SLOTS), side_by_side([near_ref, before_ref, after_ref]))
    product_far = products_of(left_far_ref[...].reshape(512, SLOTS), far_ref[...].reshape(128, SLOTS))

    @pl.when(step == 0)
    def _():
        total[...] = product
        total_far[...] = product_far

    @pl.when(step == 1)
    def _():
        pick = selector(me_ref, 512, None)
        table = exact(exact(pick, matched(total[...] + product), False), selector(me_ref, 384, (0, 1, 3)), True)
        table += exact(
            exact(pick, matched(total_far[...] + product_far), False), selector(me_ref, 128, (0,)), True
        )
        out_ref[...] = complex_lanes(table, 32)


def gram_call(kernel, me, operands, starts, scratch, name):
    def spec(operand, start):
        return pl.BlockSpec((operand.shape[0], 1, 2, 2, 16, SLOTS), lambda g: (0, start + g, 0, 0, 0, 0))

    return pl.pallas_call(
        kernel,
        grid=(2,),
        in_specs=[pl.BlockSpec(memory_space=pltpu.SMEM)] + [spec(operand, start) for operand, start in zip(operands, starts)],
        out_specs=pl.BlockSpec((16, 128), lambda g: (0, 0)),
        out_shape=jax.ShapeDtypeStruct((16, 128), jnp.float32),
        scratch_shapes=[pltpu.VMEM(shape, jnp.float32) for shape in scratch],
        compiler_params=pltpu.CompilerParams(vmem_limit_bytes=60 * MIB),
        cost_estimate=pl.CostEstimate(flops=2_000_000_000, bytes_accessed=8_000_000, transcendentals=0),
        name=name,
    )(me, *operands)


def twofold_kernel(in_ref, out_ref):
    for half in range(2):
        out_ref[half, :, 0] = in_ref[half]
        out_ref[half, :, 1] = in_ref[1 - half]


def twofold_call(blocks):
    count = 2
    result = pl.pallas_call(
        twofold_kernel,
        grid=(4 // count,),
        in_specs=[pl.BlockSpec((2, count, 128, SLOTS), lambda i: (0, i, 0, 0))],
        out_specs=pl.BlockSpec((2, count, 2, 128, SLOTS), lambda i: (0, i, 0, 0, 0)),
        out_shape=jax.ShapeDtypeStruct((2, 4, 2, 128, SLOTS), jnp.bfloat16),
        compiler_params=pltpu.CompilerParams(vmem_limit_bytes=60 * MIB),
        cost_estimate=pl.CostEstimate(flops=0, bytes_accessed=12_000_000, transcendentals=0),
        name="twofold",
    )(blocks.reshape(2, 4, 128, SLOTS))
    return result.reshape(8, 256, SLOTS)


def summed(values, axis, steps, tied=None):
    size = lax.axis_size(axis)
    for step in steps:
        received = lax.ppermute(values, axis, [(i, i ^ step) for i in range(size)])
        if tied is not None:
            received, tied = lax.optimization_barrier((received, tied))
        values = values + received
    return values, tied


def spread_blocks(kept, given, axis, tied, shifts):
    chip = lax.axis_index(axis) // 2
    got = lax.ppermute(given, axis, [(i, i ^ 1) for i in range(8)])
    pairs = []
    for shift in range(4):
        target = (chip + shift) % 4
        pairs.append(
            jnp.concatenate(
                [lax.dynamic_slice_in_dim(kept, target, 1, 0), lax.dynamic_slice_in_dim(got, target, 1, 0)], axis=0
            )
        )
    if tied is not None:
        tied, *pairs = lax.optimization_barrier((tied, *pairs))
    for shift in shifts:
        pairs[shift] = lax.ppermute(
            pairs[shift], axis, [(i, (i // 2 + shift) % 4 * 2 + i % 2) for i in range(8)]
        )
    return pairs, tied


def plane_kernel(
    core_ref, place_ref, count_ref, upper_ref, wire_ref, field_ref, forward_ref, backward_ref,
    out_ref, kept_ref, given_ref, grid_ref, mid_ref, back_ref, side_ref, stage_a, stage_b, list_ref, sems
):
    step = pl.program_id(0)
    lane = lax.broadcasted_iota(jnp.int32, (1, 128), 1)
    low = lane % 64 < 32
    sign = jnp.where(lane < 64, -1.0, 1.0).astype(jnp.bfloat16)

    def doubled(values):
        values = values.astype(jnp.bfloat16)
        return jnp.concatenate([values, pltpu.roll(values, 64, 1) * sign], axis=0)

    def exchange(first, second):
        return (
            jnp.where(low, first, pltpu.roll(second, 32, 1)),
            jnp.where(low, pltpu.roll(first, 96, 1), second),
        )

    @pl.when(step == 0)
    def _():
        def clear(i, carry):
            grid_ref[pl.ds(pl.multiple_of(i * 512, 512), 512), :] = jnp.zeros((512, 128), jnp.float32)
            return carry

        lax.fori_loop(0, ROWS // 512, clear, 0)
        grid_ref[pl.ds(ROWS, 8), :] = jnp.zeros((8, 128), jnp.float32)

        def group(p, total):
            def note(t, inner):
                list_ref[inner] = p * 15 + t
                return inner + 1

            return lax.fori_loop(0, count_ref[p], note, total)

        total = lax.fori_loop(0, GROUPS, group, 0)
        list_ref[total] = list_ref[total - 1]
        list_ref[total + 1] = list_ref[total - 1]
        list_ref[total + 2] = list_ref[total - 1]
        list_ref[255] = (total + 1) // 2
        eye_row = lax.broadcasted_iota(jnp.int32, (128, 128), 0)
        eye_column = lax.broadcasted_iota(jnp.int32, (128, 128), 1)
        eye = jnp.where(eye_row == eye_column, 1.0, 0.0).astype(jnp.bfloat16)

        def rows_of(entry):
            p = entry // 15
            block = wire_ref[p, :, pl.ds(pl.multiple_of((entry - p * 15) * 128, 128), 128)]
            twice = jnp.concatenate([block[0:32], block[0:32], block[32:64], block[32:64]], axis=0)
            return lax.dot_general(eye, twice, (((1,), (1,)), ((), ())), preferred_element_type=jnp.float32)

        def spread(entry, stage):
            for u in range(128):
                grid_ref[pl.ds(place_ref[entry * 128 + u], 1), :] = stage[u : u + 1, :]

        def scatter(i, carry):
            entry = list_ref[2 * i]
            entry_b = list_ref[2 * i + 1]
            entry_c = list_ref[2 * i + 2]
            stage_b[...] = rows_of(entry_b)
            spread(entry, stage_a)
            stage_a[...] = rows_of(entry_c)
            spread(entry_b, stage_b)
            return carry

        stage_a[...] = rows_of(list_ref[0])
        lax.fori_loop(0, list_ref[255], scatter, 0)

        def x_forward(i, carry):
            parts = []
            for j in range(N1):
                k = i * N1 + j
                first = grid_ref[pl.ds(pl.multiple_of(k * BOX, BOX), BOX), :]
                second = grid_ref[pl.ds(pl.multiple_of((k + HALF) * BOX, BOX), BOX), :]
                parts.append(doubled(jnp.where(low, first, second)))
            result = jnp.dot(forward_ref[...], jnp.concatenate(parts, axis=1), preferred_element_type=jnp.float32)
            for j in range(N1):
                k = i * N1 + j
                part = result[:, j * 128 : (j + 1) * 128]
                mid_ref[pl.ds(k, PAIRS, stride=PITCH), :] = part[:PAIRS]
                mid_ref[pl.ds(k + HALF, PAIRS, stride=PITCH), :] = part[PAIRS:]
            return carry

        lax.fori_loop(0, HALF // N1, x_forward, 0)

    def y_steps(i, carry):
        parts = []
        for j in range(N2):
            pair = step * PB + i * N2 + j
            base = pl.multiple_of(pair * PITCH, 8)
            first = mid_ref[pl.ds(base, HALF), :]
            second = mid_ref[pl.ds(base + HALF, HALF), :]
            even, odd = exchange(first, second)
            parts.append(doubled(jnp.concatenate([even, odd], axis=0)))
        spatial = jnp.dot(forward_ref[...], jnp.concatenate(parts, axis=1), preferred_element_type=jnp.float32)
        parts = []
        for j in range(N2):
            parts.append(doubled(spatial[:, j * 128 : (j + 1) * 128] * field_ref[i * N2 + j].astype(jnp.float32)))
        result = jnp.dot(backward_ref[...], jnp.concatenate(parts, axis=1), preferred_element_type=jnp.float32)
        for j in range(N2):
            pair = step * PB + i * N2 + j
            back_ref[pl.ds(pair, BOX, stride=PITCHB), :] = result[:, j * 128 : (j + 1) * 128]
        return carry

    lax.fori_loop(0, PB // N2, y_steps, 0)

    @pl.when(step == pl.num_programs(0) - 1)
    def _():
        def x_backward(i, carry):
            parts = []
            for j in range(N4):
                k = i * N4 + j
                first = back_ref[pl.ds(pl.multiple_of(k * PITCHB, 8), PAIRS), :]
                second = back_ref[pl.ds(pl.multiple_of((k + HALF) * PITCHB, 8), PAIRS), :]
                even, odd = exchange(first, second)
                parts.append(doubled(jnp.concatenate([even, odd], axis=0)))
            result = jnp.dot(backward_ref[...], jnp.concatenate(parts, axis=1), preferred_element_type=jnp.float32)
            for j in range(N4):
                k = i * N4 + j
                part = result[:, j * 128 : (j + 1) * 128]
                grid_ref[pl.ds(pl.multiple_of(k * BOX, BOX), BOX), :] = part
                grid_ref[pl.ds(pl.multiple_of((k + HALF) * BOX, BOX), BOX), :] = part
            return carry

        lax.fori_loop(0, HALF // N4, x_backward, 0)
        select_row = lax.broadcasted_iota(jnp.int32, (128, 128), 0)
        select_column = lax.broadcasted_iota(jnp.int32, (128, 128), 1)
        source = select_row % 64 // 32 * 64 + select_row // 64 * 32 + select_row % 32
        select = jnp.where(select_column == source, 1.0, 0.0).astype(jnp.bfloat16)
        origin = pl.multiple_of((step - (pl.num_programs(0) - 1)) * 8, 8)

        def side_of(p):
            return (p // 2 + core_ref[0]) % 2

        def gather(entry, stage):
            for u in range(128):
                stage[pl.ds(origin + u, 1), :] = grid_ref[pl.ds(place_ref[entry * 128 + u], 1), :]

        def write(entry, stage):
            p = entry // 15
            base = pl.multiple_of((entry - p * 15) * 128, 128)
            both = lax.dot_general(
                select, stage[...].astype(jnp.bfloat16), (((1,), (1,)), ((), ())), preferred_element_type=jnp.float32
            )
            upper = upper_ref[pl.ds(entry, 1), :] > 0.0
            values = jnp.where(upper, both[64:], both[:64]).astype(jnp.bfloat16)
            out_ref[p, :, pl.ds(base, 128)] = values
            side_ref[side_of(p), p // 4, p % 2, :, pl.ds(base, 128)] = values

        def pick(i, carry):
            entry = list_ref[2 * i]
            entry_b = list_ref[2 * i + 1]
            entry_c = list_ref[2 * i + 2]
            gather(entry_b, stage_b)
            write(entry, stage_a)
            gather(entry_c, stage_a)
            write(entry_b, stage_b)
            return carry

        def group(p, carry):
            def blank(t, inner):
                base = pl.multiple_of(t * 128, 128)
                blank = jnp.zeros((64, 128), jnp.bfloat16)
                out_ref[p, :, pl.ds(base, 128)] = blank
                side_ref[side_of(p), p // 4, p % 2, :, pl.ds(base, 128)] = blank
                return inner

            return lax.fori_loop(count_ref[p], SLOTS // 128, blank, carry)

        lax.fori_loop(0, GROUPS, group, 0)
        gather(list_ref[0], stage_a)
        lax.fori_loop(0, list_ref[255], pick, 0)
        copies = [
            pltpu.make_async_copy(side_ref.at[0], kept_ref, sems.at[0]),
            pltpu.make_async_copy(side_ref.at[1], given_ref, sems.at[1]),
        ]
        for copy in copies:
            copy.start()
        for copy in copies:
            copy.wait()


def plane_call(core, place, count, upper, wire, field, forward, backward):
    whole = lambda shape: pl.BlockSpec(shape, lambda i: (0,) * len(shape), pipeline_mode=pl.Buffered(1))
    return pl.pallas_call(
        plane_kernel,
        grid=(PAIRS // PB,),
        in_specs=[
            pl.BlockSpec(memory_space=pltpu.SMEM),
            pl.BlockSpec(memory_space=pltpu.SMEM),
            pl.BlockSpec(memory_space=pltpu.SMEM),
            whole((GROUPS * SLOTS // 128, 128)),
            whole((GROUPS, 64, SLOTS)),
            pl.BlockSpec((PB, GRID, 128), lambda i: (i, 0, 0)),
            whole((GRID, 2 * BOX)),
            whole((BOX, 2 * GRID)),
        ],
        out_specs=[whole((GROUPS, 64, SLOTS)), pl.BlockSpec(memory_space=pl.ANY), pl.BlockSpec(memory_space=pl.ANY)],
        out_shape=[jax.ShapeDtypeStruct((GROUPS, 64, SLOTS), jnp.bfloat16)]
        + [jax.ShapeDtypeStruct((4, 2, 64, SLOTS), jnp.bfloat16)] * 2,
        scratch_shapes=[
            pltpu.VMEM((ROWS + 8, 128), jnp.float32),
            pltpu.VMEM((PAIRS * PITCH, 128), jnp.float32),
            pltpu.VMEM((BOX * PITCHB, 128), jnp.float32),
            pltpu.VMEM((2, 4, 2, 64, SLOTS), jnp.bfloat16),
            pltpu.VMEM((128, 128), jnp.float32),
            pltpu.VMEM((128, 128), jnp.float32),
            pltpu.SMEM((256,), jnp.int32),
            pltpu.SemaphoreType.DMA((2,)),
        ],
        compiler_params=pltpu.CompilerParams(vmem_limit_bytes=62 * MIB),
        cost_estimate=pl.CostEstimate(flops=13_000_000_000, bytes_accessed=24_000_000, transcendentals=0),
        name="planes",
    )(core, place, count, upper, wire, field, forward, backward)


def field_kernel(lower_ref, upper_ref, out_ref):
    blank = jnp.zeros((1, lower_ref.shape[-1]), jnp.float32)
    lower = jnp.concatenate([lower_ref[...], blank], axis=0).astype(jnp.bfloat16)
    upper = jnp.concatenate([upper_ref[...], blank], axis=0).astype(jnp.bfloat16)
    once = jnp.concatenate([lower, lower, upper, upper], axis=0)
    out_ref[...] = jnp.concatenate([once, once], axis=0).T.reshape(PB, GRID, 128)


def field_call(potential):
    lanes = PB * GRID
    return pl.pallas_call(
        field_kernel,
        grid=(PAIRS // PB,),
        in_specs=[
            pl.BlockSpec((PLANES, lanes), lambda i: (0, i)),
            pl.BlockSpec((PLANES, lanes), lambda i: (0, i + PAIRS // PB)),
        ],
        out_specs=pl.BlockSpec((PB, GRID, 128), lambda i: (i, 0, 0)),
        out_shape=jax.ShapeDtypeStruct((PAIRS, GRID, 128), jnp.bfloat16),
        compiler_params=pltpu.CompilerParams(vmem_limit_bytes=60 * MIB),
        cost_estimate=pl.CostEstimate(flops=0, bytes_accessed=18_000_000, transcendentals=0),
        name="field",
    )(potential, potential)


def local(orbitals, potential, stick_column, column_slot):
    z_forward, z_backward, forward, backward = (jnp.asarray(table) for table in tables())
    live_all = stick_column >= 0
    own = lax.dynamic_slice_in_dim(stick_column, lax.axis_index("fft") * SLOTS, SLOTS)
    live = (own >= 0).astype(jnp.float32)[None, :]
    column_x, column_y = stick_column // GRID, stick_column % GRID
    box_x = jnp.where(column_x < GRID // 2, column_x + HALF, column_x - (GRID - HALF))
    box_y = jnp.where(column_y < GRID // 2, column_y + HALF, column_y - (GRID - HALF))
    place = jnp.where(live_all, box_y * BOX + box_x, ROWS)
    count = (jnp.sum(live_all.reshape(GROUPS, SLOTS).astype(jnp.int32), axis=1) + 127) // 128
    upper = (live_all & (box_y >= HALF)).astype(jnp.float32).reshape(GROUPS * SLOTS // 128, 128)
    me = lax.axis_index("band").astype(jnp.int32)[None]
    core = me % 2

    wire, kept, given = z_forward_call(core, orbitals.transpose(0, 2, 1), live, z_forward)
    incoming = lax.all_to_all(wire.reshape(GROUPS, 64, SLOTS), "fft", split_axis=0, concat_axis=0, tiled=True)
    shares, potential = spread_blocks(kept, given, "band", potential, (1, 2, 3))
    field = field_call(potential)
    incoming, field, place, count, upper, *shares = lax.optimization_barrier(
        (incoming, field, place, count, upper, *shares)
    )
    left = lax.all_to_all(twofold_call(incoming), "band", split_axis=0, concat_axis=0, tiled=True)
    left = left.reshape(8, 4, 2, 2, 16, SLOTS)
    outgoing, kept, given = plane_call(core, place, count, upper, incoming, field, forward, backward)
    returned = lax.all_to_all(outgoing, "fft", split_axis=0, concat_axis=0, tiled=True)
    split = (4, 2, 2, 2, 16, SLOTS)
    (near, before, opposite, after), _ = spread_blocks(
        kept.reshape(split), given.reshape(split), "band", None, (1, 3)
    )
    product_s = gram_call(overlap_kernel, me, shares, (0, 0, 0, 0), [(512, 512)], "overlap")
    product_h = gram_call(
        hamiltonian_kernel,
        me,
        [left, left, near, before, after, opposite],
        (0, 2, 0, 0, 0, 0),
        [(512, 384), (512, 128)],
        "hamiltonian",
    )
    applied = z_backward_call(returned.reshape(GROUPS, 2, 2, ZPAD, SLOTS), live, z_backward)
    products, _ = summed(product_s + product_h, "band", (1, 2, 4))
    products, _ = summed(products, "fft", (1, 2))
    products, applied = summed(products, "fft", (4,), applied)
    products, _ = summed(products, "fft", (8,))
    products = products * (1.0 / (2.0 * STICKS * GRID))
    products = products[:, :64].reshape(16, 4, 16).transpose(1, 0, 2)
    return (applied.transpose(0, 2, 1), products[0:2], products[2:4])


def solution(mesh):
    return jax.shard_map(
        local,
        mesh=mesh,
        in_specs=(P("band", "fft", None), P("fft", None), P(), P()),
        out_specs=(P("band", "fft", None), P(), P()),
        check_vma=False,
    )
```

```python
import functools
import math

import jax
import jax.numpy as jnp
import ml_dtypes
import numpy as np
from jax import lax
from jax.experimental import pallas as pl
from jax.experimental.pallas import tpu as pltpu
from jax.sharding import PartitionSpec as P

STICKS = 24576
GRID = 240
SLOTS = 1920
GROUPS = 16
PLANES = 15
ZPAD = 16
BOX = 192
HALF = BOX // 2
PAIRS = GRID // 2
ROWS = BOX * BOX
PITCH = 200
PITCHB = 120
PB = 24
N1 = 8
N2 = 12
N4 = 8
MIB = 1 << 20


def trig():
    counter = np.arange(GRID, dtype=np.int32)
    phases = counter[:, None] * counter[None, :] % GRID
    angles = phases.astype(np.float32) * np.float32(2.0 * math.pi / GRID)
    factor = np.float32(1.0 / math.sqrt(GRID))
    cosine = (np.cos(angles) * factor).astype(ml_dtypes.bfloat16)
    sine = (np.sin(angles) * factor).astype(ml_dtypes.bfloat16)
    return cosine, sine


def tables():
    cosine, sine = trig()
    box = np.arange(BOX) - HALF
    box = np.where(box < 0, box + GRID, box)
    z_forward = np.zeros((GROUPS, 2, ZPAD, 2, GRID), ml_dtypes.bfloat16)
    cos_z = cosine.reshape(GROUPS, PLANES, GRID)
    sin_z = sine.reshape(GROUPS, PLANES, GRID)
    z_forward[:, 0, :PLANES, 0] = cos_z
    z_forward[:, 0, :PLANES, 1] = -sin_z
    z_forward[:, 1, :PLANES, 0] = sin_z
    z_forward[:, 1, :PLANES, 1] = cos_z
    z_forward = z_forward.reshape(GROUPS * 2 * ZPAD, 2 * GRID)
    z_backward = np.ascontiguousarray(z_forward.T)
    cos_box, sin_box = cosine[:, box], sine[:, box]
    forward = np.concatenate([cos_box, sin_box], axis=1)
    backward = np.concatenate([cos_box.T, -sin_box.T], axis=1)
    return z_forward, z_backward, forward, backward


def z_forward_kernel(core_ref, orbit_ref, live_ref, table_ref, wire_ref, kept_ref, given_ref, masked_ref):
    masked_ref[...] = (orbit_ref[0].astype(jnp.float32) * live_ref[...]).astype(jnp.bfloat16)
    for core in range(2):

        @pl.when(core_ref[0] == core)
        def _():
            for q in range(15):
                target = kept_ref if q // 2 % 2 == core else given_ref
                for c in range(2):
                    start = c * GRID + q * 16
                    target[q // 4, q % 2, c, 0] = masked_ref[start : start + 16]
            target = kept_ref if core == 1 else given_ref
            for c in range(2):
                target[3, 1, c, 0] = jnp.zeros((16, SLOTS), jnp.bfloat16)

    values = jnp.dot(table_ref[...], masked_ref[...], preferred_element_type=jnp.float32).astype(jnp.bfloat16)
    wire_ref[...] = values.reshape(GROUPS, 2, 1, ZPAD, SLOTS)


def z_forward_call(core, orbits, live, table):
    share = pl.BlockSpec((4, 2, 2, 1, 16, SLOTS), lambda b: (0, 0, 0, b, 0, 0))
    return pl.pallas_call(
        z_forward_kernel,
        grid=(2,),
        in_specs=[
            pl.BlockSpec(memory_space=pltpu.SMEM),
            pl.BlockSpec((1, 2 * GRID, SLOTS), lambda b: (b, 0, 0)),
            pl.BlockSpec((1, SLOTS), lambda b: (0, 0)),
            pl.BlockSpec((512, 2 * GRID), lambda b: (0, 0)),
        ],
        out_specs=[pl.BlockSpec((GROUPS, 2, 1, ZPAD, SLOTS), lambda b: (0, 0, b, 0, 0)), share, share],
        out_shape=[jax.ShapeDtypeStruct((GROUPS, 2, 2, ZPAD, SLOTS), jnp.bfloat16)]
        + [jax.ShapeDtypeStruct((4, 2, 2, 2, 16, SLOTS), jnp.bfloat16)] * 2,
        scratch_shapes=[pltpu.VMEM((2 * GRID, SLOTS), jnp.bfloat16)],
        compiler_params=pltpu.CompilerParams(vmem_limit_bytes=60 * MIB),
        cost_estimate=pl.CostEstimate(flops=1_800_000_000, bytes_accessed=12_000_000, transcendentals=0),
        name="z_forward",
    )(core, orbits, live, table)


def z_backward_kernel(wire_ref, live_ref, table_ref, out_ref):
    values = wire_ref[...].reshape(512, SLOTS)
    applied = jnp.dot(table_ref[...], values, preferred_element_type=jnp.float32)
    out_ref[0] = (applied * live_ref[...]).astype(jnp.bfloat16)


def z_backward_call(wire, live, table):
    return pl.pallas_call(
        z_backward_kernel,
        grid=(2,),
        in_specs=[
            pl.BlockSpec((GROUPS, 2, 1, ZPAD, SLOTS), lambda b: (0, 0, b, 0, 0)),
            pl.BlockSpec((1, SLOTS), lambda b: (0, 0)),
            pl.BlockSpec((2 * GRID, 512), lambda b: (0, 0)),
        ],
        out_specs=pl.BlockSpec((1, 2 * GRID, SLOTS), lambda b: (b, 0, 0)),
        out_shape=jax.ShapeDtypeStruct((2, 2 * GRID, SLOTS), jnp.bfloat16),
        compiler_params=pltpu.CompilerParams(vmem_limit_bytes=60 * MIB),
        cost_estimate=pl.CostEstimate(flops=1_800_000_000, bytes_accessed=8_000_000, transcendentals=0),
        name="z_backward",
    )(wire, live, table)


def side_by_side(refs):
    return jnp.concatenate([ref[...].reshape(-1, SLOTS) for ref in refs], axis=0)


def products_of(left, right):
    return lax.dot_general(left, right, (((1,), (1,)), ((), ())), preferred_element_type=jnp.float32)


def exact(left, right, transposed):
    dims = (((1,), (1 if transposed else 0,)), ((), ()))
    return lax.dot_general(left, right, dims, preferred_element_type=jnp.float32, precision=lax.Precision.HIGHEST)


def selector(me_ref, size, shifts):
    row = lax.broadcasted_iota(jnp.int32, (32, size), 0)
    index = lax.broadcasted_iota(jnp.int32, (32, size), 1)
    source = index // 64
    if shifts is not None:
        shift = source // 2
        for position, value in enumerate(shifts):
            shift = jnp.where(source // 2 == position, value, shift)
        source = (me_ref[0] // 2 + 4 - shift) % 4 * 2 + (me_ref[0] + source) % 2
    band = source * 2 + index // 16 % 2
    return jnp.where((row % 16 == band) & (row // 16 == index // 32 % 2), 1.0, 0.0)


def matched(total):
    row = lax.broadcasted_iota(jnp.int32, total.shape, 0)
    column = lax.broadcasted_iota(jnp.int32, total.shape, 1)
    return jnp.where(row % 16 == column % 16, total, 0.0)


def complex_lanes(table, first_lane):
    row = lax.broadcasted_iota(jnp.int32, (32, 128), 0)
    lane = lax.broadcasted_iota(jnp.int32, (32, 128), 1) - first_lane
    match = (lane >= 0) & (lane < 32) & (lane % 16 == row % 16)
    second, imag = lane // 16 == 1, row // 16 == 1
    with_real = jnp.where(match & (second == imag), 1.0, 0.0)
    with_imag = jnp.where(match & (second != imag), jnp.where(second, -1.0, 1.0), 0.0)
    return exact(table[:16], with_real, False) + exact(table[16:], with_imag, False)


def overlap_kernel(me_ref, *refs):
    *piece_refs, out_ref, total = refs
    step = pl.program_id(0)
    values = side_by_side(piece_refs)
    product = products_of(values, values)

    @pl.when(step == 0)
    def _():
        total[...] = product

    @pl.when(step == 1)
    def _():
        pick = selector(me_ref, 512, (0, 1, 2, 3))
        table = exact(exact(pick, matched(total[...] + product), False), pick, True)
        out_ref[...] = complex_lanes(table, 0)


def near_kernel(me_ref, left_ref, left_far_ref, kept_near, got_near, kept_far, got_far, out_ref, total):
    step = pl.program_id(0)
    product = products_of(left_ref[...].reshape(512, SLOTS), side_by_side([kept_near, got_near]))
    product += products_of(left_far_ref[...].reshape(512, SLOTS), side_by_side([kept_far, got_far]))

    @pl.when(step == 0)
    def _():
        total[...] = product

    @pl.when(step == 1)
    def _():
        pick = selector(me_ref, 512, None)
        table = exact(exact(pick, matched(total[...] + product), False), selector(me_ref, 128, (0,)), True)
        out_ref[...] = complex_lanes(table, 32)


def next_kernel(me_ref, left_ref, before_same, before_other, after_same, after_other, out_ref, total):
    step = pl.program_id(0)
    product = products_of(
        left_ref[...].reshape(512, SLOTS), side_by_side([before_same, before_other, after_same, after_other])
    )

    @pl.when(step == 0)
    def _():
        total[...] = product

    @pl.when(step == 1)
    def _():
        pick = selector(me_ref, 512, None)
        table = exact(exact(pick, matched(total[...] + product), False), selector(me_ref, 256, (1, 3)), True)
        out_ref[...] = complex_lanes(table, 32)


def gram_call(kernel, me, operands, shape, name):
    def spec(operand):
        _, size, block, start = operand
        return pl.BlockSpec((size, 1, 2, 2, 16, SLOTS), lambda g: (block, start + g, 0, 0, 0, 0))

    return pl.pallas_call(
        kernel,
        grid=(2,),
        in_specs=[pl.BlockSpec(memory_space=pltpu.SMEM)] + [spec(operand) for operand in operands],
        out_specs=pl.BlockSpec((16, 128), lambda g: (0, 0)),
        out_shape=jax.ShapeDtypeStruct((16, 128), jnp.float32),
        scratch_shapes=[pltpu.VMEM(shape, jnp.float32)],
        compiler_params=pltpu.CompilerParams(vmem_limit_bytes=60 * MIB),
        cost_estimate=pl.CostEstimate(flops=2_000_000_000, bytes_accessed=8_000_000, transcendentals=0),
        name=name,
    )(me, *[operand[0] for operand in operands])


def twofold_kernel(in_ref, out_ref):
    for half in range(2):
        out_ref[half, :, 0] = in_ref[half]
        out_ref[half, :, 1] = in_ref[1 - half]


def twofold_call(blocks):
    count = 2
    result = pl.pallas_call(
        twofold_kernel,
        grid=(4 // count,),
        in_specs=[pl.BlockSpec((2, count, 128, SLOTS), lambda i: (0, i, 0, 0))],
        out_specs=pl.BlockSpec((2, count, 2, 128, SLOTS), lambda i: (0, i, 0, 0, 0)),
        out_shape=jax.ShapeDtypeStruct((2, 4, 2, 128, SLOTS), jnp.bfloat16),
        compiler_params=pltpu.CompilerParams(vmem_limit_bytes=60 * MIB),
        cost_estimate=pl.CostEstimate(flops=0, bytes_accessed=12_000_000, transcendentals=0),
        name="twofold",
    )(blocks.reshape(2, 4, 128, SLOTS))
    return result.reshape(8, 256, SLOTS)


def summed(values, axis, steps, tied=None):
    size = lax.axis_size(axis)
    for step in steps:
        received = lax.ppermute(values, axis, [(i, i ^ step) for i in range(size)])
        if tied is not None:
            received, tied = lax.optimization_barrier((received, tied))
        values = values + received
    return values, tied


def moved(values, shift, other):
    return lax.ppermute(
        values, "band", [(i, (i // 2 + shift) % 4 * 2 + (i % 2 + other) % 2) for i in range(8)]
    )


def spread_blocks(kept, given, tied):
    chip = lax.axis_index("band") // 2
    got = moved(given, 0, 1)
    pairs = []
    for shift in range(4):
        target = (chip + shift) % 4
        pairs.append(
            jnp.concatenate(
                [lax.dynamic_slice_in_dim(kept, target, 1, 0), lax.dynamic_slice_in_dim(got, target, 1, 0)], axis=0
            )
        )
    tied, *pairs = lax.optimization_barrier((tied, *pairs))
    return [pairs[0]] + [moved(pairs[shift], shift, 0) for shift in (1, 2, 3)], tied


def plane_kernel(
    me_ref, place_ref, count_ref, upper_ref, wire_hbm, field_ref, forward_ref, backward_ref,
    out_ref, kept_ref, given_ref, next_same, next_other, last_same, last_other, grid_ref, mid_ref, back_ref, side_ref, wire_ref, stage_a, stage_b, list_ref, sems
):
    step = pl.program_id(0)
    lane = lax.broadcasted_iota(jnp.int32, (1, 128), 1)
    low = lane % 64 < 32
    sign = jnp.where(lane < 64, -1.0, 1.0).astype(jnp.bfloat16)

    def doubled(values):
        values = values.astype(jnp.bfloat16)
        return jnp.concatenate([values, pltpu.roll(values, 64, 1) * sign], axis=0)

    def exchange(first, second):
        return (
            jnp.where(low, first, pltpu.roll(second, 32, 1)),
            jnp.where(low, pltpu.roll(first, 96, 1), second),
        )

    @pl.when(step == 0)
    def _():
        fetch = pltpu.make_async_copy(wire_hbm, wire_ref, sems.at[0])
        fetch.start()

        def clear(i, carry):
            grid_ref[pl.ds(pl.multiple_of(i * 512, 512), 512), :] = jnp.zeros((512, 128), jnp.float32)
            return carry

        lax.fori_loop(0, ROWS // 512, clear, 0)
        grid_ref[pl.ds(ROWS, 8), :] = jnp.zeros((8, 128), jnp.float32)

        def group(p, total):
            def note(t, inner):
                list_ref[inner] = p * 15 + t
                return inner + 1

            return lax.fori_loop(0, count_ref[p], note, total)

        total = lax.fori_loop(0, GROUPS, group, 0)
        list_ref[total] = list_ref[total - 1]
        list_ref[total + 1] = list_ref[total - 1]
        list_ref[total + 2] = list_ref[total - 1]
        list_ref[255] = (total + 1) // 2
        eye_row = lax.broadcasted_iota(jnp.int32, (128, 128), 0)
        eye_column = lax.broadcasted_iota(jnp.int32, (128, 128), 1)
        eye = jnp.where(eye_row == eye_column, 1.0, 0.0).astype(jnp.bfloat16)

        def rows_of(entry):
            p = entry // 15
            block = wire_ref[p, :, pl.ds(pl.multiple_of((entry - p * 15) * 128, 128), 128)]
            twice = jnp.concatenate([block[0:32], block[0:32], block[32:64], block[32:64]], axis=0)
            return lax.dot_general(eye, twice, (((1,), (1,)), ((), ())), preferred_element_type=jnp.float32)

        def spread(entry, stage):
            for u in range(128):
                grid_ref[pl.ds(place_ref[entry * 128 + u], 1), :] = stage[u : u + 1, :]

        def scatter(i, carry):
            entry = list_ref[2 * i]
            entry_b = list_ref[2 * i + 1]
            entry_c = list_ref[2 * i + 2]
            stage_b[...] = rows_of(entry_b)
            spread(entry, stage_a)
            stage_a[...] = rows_of(entry_c)
            spread(entry_b, stage_b)
            return carry

        fetch.wait()
        stage_a[...] = rows_of(list_ref[0])
        lax.fori_loop(0, list_ref[255], scatter, 0)

        def x_forward(i, carry):
            parts = []
            for j in range(N1):
                k = i * N1 + j
                first = grid_ref[pl.ds(pl.multiple_of(k * BOX, BOX), BOX), :]
                second = grid_ref[pl.ds(pl.multiple_of((k + HALF) * BOX, BOX), BOX), :]
                parts.append(doubled(jnp.where(low, first, second)))
            result = jnp.dot(forward_ref[...], jnp.concatenate(parts, axis=1), preferred_element_type=jnp.float32)
            for j in range(N1):
                k = i * N1 + j
                part = result[:, j * 128 : (j + 1) * 128]
                mid_ref[pl.ds(k, PAIRS, stride=PITCH), :] = part[:PAIRS]
                mid_ref[pl.ds(k + HALF, PAIRS, stride=PITCH), :] = part[PAIRS:]
            return carry

        lax.fori_loop(0, HALF // N1, x_forward, 0)

    def y_steps(i, carry):
        parts = []
        for j in range(N2):
            pair = step * PB + i * N2 + j
            base = pl.multiple_of(pair * PITCH, 8)
            first = mid_ref[pl.ds(base, HALF), :]
            second = mid_ref[pl.ds(base + HALF, HALF), :]
            even, odd = exchange(first, second)
            parts.append(doubled(jnp.concatenate([even, odd], axis=0)))
        spatial = jnp.dot(forward_ref[...], jnp.concatenate(parts, axis=1), preferred_element_type=jnp.float32)
        parts = []
        for j in range(N2):
            parts.append(doubled(spatial[:, j * 128 : (j + 1) * 128] * field_ref[i * N2 + j].astype(jnp.float32)))
        result = jnp.dot(backward_ref[...], jnp.concatenate(parts, axis=1), preferred_element_type=jnp.float32)
        for j in range(N2):
            pair = step * PB + i * N2 + j
            back_ref[pl.ds(pair, BOX, stride=PITCHB), :] = result[:, j * 128 : (j + 1) * 128]
        return carry

    lax.fori_loop(0, PB // N2, y_steps, 0)

    @pl.when(step == pl.num_programs(0) - 1)
    def _():
        def x_backward(i, carry):
            parts = []
            for j in range(N4):
                k = i * N4 + j
                first = back_ref[pl.ds(pl.multiple_of(k * PITCHB, 8), PAIRS), :]
                second = back_ref[pl.ds(pl.multiple_of((k + HALF) * PITCHB, 8), PAIRS), :]
                even, odd = exchange(first, second)
                parts.append(doubled(jnp.concatenate([even, odd], axis=0)))
            result = jnp.dot(backward_ref[...], jnp.concatenate(parts, axis=1), preferred_element_type=jnp.float32)
            for j in range(N4):
                k = i * N4 + j
                part = result[:, j * 128 : (j + 1) * 128]
                grid_ref[pl.ds(pl.multiple_of(k * BOX, BOX), BOX), :] = part
                grid_ref[pl.ds(pl.multiple_of((k + HALF) * BOX, BOX), BOX), :] = part
            return carry

        lax.fori_loop(0, HALF // N4, x_backward, 0)
        select_row = lax.broadcasted_iota(jnp.int32, (128, 128), 0)
        select_column = lax.broadcasted_iota(jnp.int32, (128, 128), 1)
        source = select_row % 64 // 32 * 64 + select_row // 64 * 32 + select_row % 32
        select = jnp.where(select_column == source, 1.0, 0.0).astype(jnp.bfloat16)
        origin = pl.multiple_of((step - (pl.num_programs(0) - 1)) * 8, 8)

        def side_of(p):
            return (p // 2 + me_ref[0]) % 2

        def gather(entry, stage):
            for u in range(128):
                stage[pl.ds(origin + u, 1), :] = grid_ref[pl.ds(place_ref[entry * 128 + u], 1), :]

        def write(entry, stage):
            p = entry // 15
            base = pl.multiple_of((entry - p * 15) * 128, 128)
            both = lax.dot_general(
                select, stage[...].astype(jnp.bfloat16), (((1,), (1,)), ((), ())), preferred_element_type=jnp.float32
            )
            upper = upper_ref[pl.ds(entry, 1), :] > 0.0
            values = jnp.where(upper, both[64:], both[:64]).astype(jnp.bfloat16)
            out_ref[p, :, pl.ds(base, 128)] = values
            side_ref[side_of(p), p // 4, p % 2, :, pl.ds(base, 128)] = values

        def pick(i, carry):
            entry = list_ref[2 * i]
            entry_b = list_ref[2 * i + 1]
            entry_c = list_ref[2 * i + 2]
            gather(entry_b, stage_b)
            write(entry, stage_a)
            gather(entry_c, stage_a)
            write(entry_b, stage_b)
            return carry

        def group(p, carry):
            def blank(t, inner):
                base = pl.multiple_of(t * 128, 128)
                blank = jnp.zeros((64, 128), jnp.bfloat16)
                out_ref[p, :, pl.ds(base, 128)] = blank
                side_ref[side_of(p), p // 4, p % 2, :, pl.ds(base, 128)] = blank
                return inner

            return lax.fori_loop(count_ref[p], SLOTS // 128, blank, carry)

        lax.fori_loop(0, GROUPS, group, 0)
        gather(list_ref[0], stage_a)
        lax.fori_loop(0, list_ref[255], pick, 0)
        chip = me_ref[0] // 2
        after, far, before = (chip + 1) % 4, (chip + 2) % 4, (chip + 3) % 4
        routes = [
            (side_ref.at[0, after], next_same),
            (side_ref.at[1, after], next_other),
            (side_ref.at[0, before], last_same),
            (side_ref.at[1, before], last_other),
            (side_ref.at[1, chip], given_ref.at[0]),
            (side_ref.at[1, far], given_ref.at[1]),
            (side_ref.at[0, chip], kept_ref.at[0]),
            (side_ref.at[0, far], kept_ref.at[1]),
        ]
        copies = [pltpu.make_async_copy(*route, sems.at[1 + n]) for n, route in enumerate(routes)]
        for copy in copies:
            copy.start()
        for copy in copies:
            copy.wait()


def plane_call(me, place, count, upper, wire, field, forward, backward):
    whole = lambda shape: pl.BlockSpec(shape, lambda i: (0,) * len(shape), pipeline_mode=pl.Buffered(1))
    return pl.pallas_call(
        plane_kernel,
        grid=(PAIRS // PB,),
        in_specs=[
            pl.BlockSpec(memory_space=pltpu.SMEM),
            pl.BlockSpec(memory_space=pltpu.SMEM),
            pl.BlockSpec(memory_space=pltpu.SMEM),
            whole((GROUPS * SLOTS // 128, 128)),
            pl.BlockSpec(memory_space=pl.ANY),
            pl.BlockSpec((PB, GRID, 128), lambda i: (i, 0, 0)),
            whole((GRID, 2 * BOX)),
            whole((BOX, 2 * GRID)),
        ],
        out_specs=[whole((GROUPS, 64, SLOTS))] + [pl.BlockSpec(memory_space=pl.ANY)] * 6,
        out_shape=[jax.ShapeDtypeStruct((GROUPS, 64, SLOTS), jnp.bfloat16)]
        + [jax.ShapeDtypeStruct((2, 2, 64, SLOTS), jnp.bfloat16)] * 2
        + [jax.ShapeDtypeStruct((2, 64, SLOTS), jnp.bfloat16)] * 4,
        scratch_shapes=[
            pltpu.VMEM((ROWS + 8, 128), jnp.float32),
            pltpu.VMEM((PAIRS * PITCH, 128), jnp.float32),
            pltpu.VMEM((BOX * PITCHB, 128), jnp.float32),
            pltpu.VMEM((2, 4, 2, 64, SLOTS), jnp.bfloat16),
            pltpu.VMEM((GROUPS, 64, SLOTS), jnp.bfloat16),
            pltpu.VMEM((128, 128), jnp.float32),
            pltpu.VMEM((128, 128), jnp.float32),
            pltpu.SMEM((256,), jnp.int32),
            pltpu.SemaphoreType.DMA((9,)),
        ],
        compiler_params=pltpu.CompilerParams(vmem_limit_bytes=62 * MIB),
        cost_estimate=pl.CostEstimate(flops=13_000_000_000, bytes_accessed=24_000_000, transcendentals=0),
        name="planes",
    )(me, place, count, upper, wire, field, forward, backward)


def field_kernel(lower_ref, upper_ref, out_ref):
    blank = jnp.zeros((1, lower_ref.shape[-1]), jnp.float32)
    lower = jnp.concatenate([lower_ref[...], blank], axis=0).astype(jnp.bfloat16)
    upper = jnp.concatenate([upper_ref[...], blank], axis=0).astype(jnp.bfloat16)
    once = jnp.concatenate([lower, lower, upper, upper], axis=0)
    out_ref[...] = jnp.concatenate([once, once], axis=0).T.reshape(PB, GRID, 128)


def field_call(potential):
    lanes = PB * GRID
    return pl.pallas_call(
        field_kernel,
        grid=(PAIRS // PB,),
        in_specs=[
            pl.BlockSpec((PLANES, lanes), lambda i: (0, i)),
            pl.BlockSpec((PLANES, lanes), lambda i: (0, i + PAIRS // PB)),
        ],
        out_specs=pl.BlockSpec((PB, GRID, 128), lambda i: (i, 0, 0)),
        out_shape=jax.ShapeDtypeStruct((PAIRS, GRID, 128), jnp.bfloat16),
        compiler_params=pltpu.CompilerParams(vmem_limit_bytes=60 * MIB),
        cost_estimate=pl.CostEstimate(flops=0, bytes_accessed=18_000_000, transcendentals=0),
        name="field",
    )(potential, potential)


def local(orbitals, potential, stick_column, column_slot):
    z_forward, z_backward, forward, backward = (jnp.asarray(table) for table in tables())
    live_all = stick_column >= 0
    own = lax.dynamic_slice_in_dim(stick_column, lax.axis_index("fft") * SLOTS, SLOTS)
    live = (own >= 0).astype(jnp.float32)[None, :]
    column_x, column_y = stick_column // GRID, stick_column % GRID
    box_x = jnp.where(column_x < GRID // 2, column_x + HALF, column_x - (GRID - HALF))
    box_y = jnp.where(column_y < GRID // 2, column_y + HALF, column_y - (GRID - HALF))
    place = jnp.where(live_all, box_y * BOX + box_x, ROWS)
    count = (jnp.sum(live_all.reshape(GROUPS, SLOTS).astype(jnp.int32), axis=1) + 127) // 128
    upper = (live_all & (box_y >= HALF)).astype(jnp.float32).reshape(GROUPS * SLOTS // 128, 128)
    me = lax.axis_index("band").astype(jnp.int32)[None]
    core = me % 2

    wire, kept, given = z_forward_call(core, orbitals.transpose(0, 2, 1), live, z_forward)
    incoming = lax.all_to_all(wire.reshape(GROUPS, 64, SLOTS), "fft", split_axis=0, concat_axis=0, tiled=True)
    shares, potential = spread_blocks(kept, given, potential)
    field = field_call(potential)
    incoming, field, place, count, upper, *shares = lax.optimization_barrier(
        (incoming, field, place, count, upper, *shares)
    )
    left = lax.all_to_all(twofold_call(incoming), "band", split_axis=0, concat_axis=0, tiled=True)
    left = left.reshape(8, 4, 2, 2, 16, SLOTS)
    outgoing, kept, given, *sides = plane_call(me, place, count, upper, incoming, field, forward, backward)
    piece = (1, 2, 2, 2, 16, SLOTS)
    sides = [side.reshape(piece) for side in sides]
    arrived = [moved(side, shift, other) for side, (shift, other) in zip(sides, ((1, 0), (1, 1), (3, 0), (3, 1)))]
    kept, got = kept.reshape(2, 2, 2, 2, 16, SLOTS), moved(given.reshape(2, 2, 2, 2, 16, SLOTS), 0, 1)
    returned = lax.all_to_all(outgoing, "fft", split_axis=0, concat_axis=0, tiled=True)
    products = gram_call(overlap_kernel, me, [(share, 2, 0, 0) for share in shares], (512, 512), "overlap")
    lefts = [(left, 8, 0, 0), (left, 8, 0, 2)]
    nears = [(kept, 1, 0, 0), (got, 1, 0, 0), (kept, 1, 1, 0), (got, 1, 1, 0)]
    products += gram_call(near_kernel, me, lefts + nears, (512, 128), "near")
    products += gram_call(next_kernel, me, lefts[:1] + [(side, 1, 0, 0) for side in arrived], (512, 256), "next")
    applied = z_backward_call(returned.reshape(GROUPS, 2, 2, ZPAD, SLOTS), live, z_backward)
    products, _ = summed(products, "band", (1, 2, 4))
    products, _ = summed(products, "fft", (1, 2))
    products, applied = summed(products, "fft", (4,), applied)
    products, _ = summed(products, "fft", (8,))
    products = products * (1.0 / (2.0 * STICKS * GRID))
    products = products[:, :64].reshape(16, 4, 16).transpose(1, 0, 2)
    return (applied.transpose(0, 2, 1), products[0:2], products[2:4])


def solution(mesh):
    return jax.shard_map(
        local,
        mesh=mesh,
        in_specs=(P("band", "fft", None), P("fft", None), P(), P()),
        out_specs=(P("band", "fft", None), P(), P()),
        check_vma=False,
    )
```

```python
import functools
import math

import jax
import jax.numpy as jnp
import ml_dtypes
import numpy as np
from jax import lax
from jax.experimental import pallas as pl
from jax.experimental.pallas import tpu as pltpu
from jax.sharding import PartitionSpec as P

STICKS = 24576
GRID = 240
SLOTS = 1920
GROUPS = 16
PLANES = 15
ZPAD = 16
BOX = 192
HALF = BOX // 2
PAIRS = GRID // 2
ROWS = BOX * BOX
PITCH = 200
PITCHB = 120
PB = 24
N1 = 12
N2 = 12
N4 = 12
MIB = 1 << 20


def trig():
    counter = np.arange(GRID, dtype=np.int32)
    phases = counter[:, None] * counter[None, :] % GRID
    angles = phases.astype(np.float32) * np.float32(2.0 * math.pi / GRID)
    factor = np.float32(1.0 / math.sqrt(GRID))
    cosine = (np.cos(angles) * factor).astype(ml_dtypes.bfloat16)
    sine = (np.sin(angles) * factor).astype(ml_dtypes.bfloat16)
    return cosine, sine


def tables():
    cosine, sine = trig()
    box = np.arange(BOX) - HALF
    box = np.where(box < 0, box + GRID, box)
    z_forward = np.zeros((GROUPS, 2, ZPAD, 2, GRID), ml_dtypes.bfloat16)
    cos_z = cosine.reshape(GROUPS, PLANES, GRID)
    sin_z = sine.reshape(GROUPS, PLANES, GRID)
    z_forward[:, 0, :PLANES, 0] = cos_z
    z_forward[:, 0, :PLANES, 1] = -sin_z
    z_forward[:, 1, :PLANES, 0] = sin_z
    z_forward[:, 1, :PLANES, 1] = cos_z
    z_forward = z_forward.reshape(GROUPS * 2 * ZPAD, 2 * GRID)
    z_backward = np.ascontiguousarray(z_forward.T)
    cos_box, sin_box = cosine[:, box], sine[:, box]
    forward = np.concatenate([cos_box, sin_box], axis=1)
    backward = np.concatenate([cos_box.T, -sin_box.T], axis=1)
    return z_forward, z_backward, forward, backward


def z_forward_kernel(core_ref, orbit_ref, live_ref, table_ref, wire_ref, kept_ref, given_ref, masked_ref):
    masked_ref[...] = (orbit_ref[0].astype(jnp.float32) * live_ref[...]).astype(jnp.bfloat16)
    for core in range(2):

        @pl.when(core_ref[0] == core)
        def _():
            for q in range(15):
                target = kept_ref if q // 2 % 2 == core else given_ref
                for c in range(2):
                    start = c * GRID + q * 16
                    target[q // 4, q % 2, c, 0] = masked_ref[start : start + 16]
            target = kept_ref if core == 1 else given_ref
            for c in range(2):
                target[3, 1, c, 0] = jnp.zeros((16, SLOTS), jnp.bfloat16)

    values = jnp.dot(table_ref[...], masked_ref[...], preferred_element_type=jnp.float32).astype(jnp.bfloat16)
    wire_ref[...] = values.reshape(GROUPS, 2, 1, ZPAD, SLOTS)


def z_forward_call(core, orbits, live, table):
    share = pl.BlockSpec((4, 2, 2, 1, 16, SLOTS), lambda b: (0, 0, 0, b, 0, 0))
    return pl.pallas_call(
        z_forward_kernel,
        grid=(2,),
        in_specs=[
            pl.BlockSpec(memory_space=pltpu.SMEM),
            pl.BlockSpec((1, 2 * GRID, SLOTS), lambda b: (b, 0, 0)),
            pl.BlockSpec((1, SLOTS), lambda b: (0, 0)),
            pl.BlockSpec((512, 2 * GRID), lambda b: (0, 0)),
        ],
        out_specs=[pl.BlockSpec((GROUPS, 2, 1, ZPAD, SLOTS), lambda b: (0, 0, b, 0, 0)), share, share],
        out_shape=[jax.ShapeDtypeStruct((GROUPS, 2, 2, ZPAD, SLOTS), jnp.bfloat16)]
        + [jax.ShapeDtypeStruct((4, 2, 2, 2, 16, SLOTS), jnp.bfloat16)] * 2,
        scratch_shapes=[pltpu.VMEM((2 * GRID, SLOTS), jnp.bfloat16)],
        compiler_params=pltpu.CompilerParams(vmem_limit_bytes=60 * MIB),
        cost_estimate=pl.CostEstimate(flops=1_800_000_000, bytes_accessed=12_000_000, transcendentals=0),
        name="z_forward",
    )(core, orbits, live, table)


def z_backward_kernel(wire_ref, live_ref, table_ref, out_ref):
    values = wire_ref[...].reshape(512, SLOTS)
    applied = jnp.dot(table_ref[...], values, preferred_element_type=jnp.float32)
    out_ref[0] = (applied * live_ref[...]).astype(jnp.bfloat16)


def z_backward_call(wire, live, table):
    return pl.pallas_call(
        z_backward_kernel,
        grid=(2,),
        in_specs=[
            pl.BlockSpec((GROUPS, 2, 1, ZPAD, SLOTS), lambda b: (0, 0, b, 0, 0)),
            pl.BlockSpec((1, SLOTS), lambda b: (0, 0)),
            pl.BlockSpec((2 * GRID, 512), lambda b: (0, 0)),
        ],
        out_specs=pl.BlockSpec((1, 2 * GRID, SLOTS), lambda b: (b, 0, 0)),
        out_shape=jax.ShapeDtypeStruct((2, 2 * GRID, SLOTS), jnp.bfloat16),
        compiler_params=pltpu.CompilerParams(vmem_limit_bytes=60 * MIB),
        cost_estimate=pl.CostEstimate(flops=1_800_000_000, bytes_accessed=8_000_000, transcendentals=0),
        name="z_backward",
    )(wire, live, table)


def side_by_side(refs):
    return jnp.concatenate([ref[...].reshape(-1, SLOTS) for ref in refs], axis=0)


def products_of(left, right):
    return lax.dot_general(left, right, (((1,), (1,)), ((), ())), preferred_element_type=jnp.float32)


def exact(left, right, transposed):
    dims = (((1,), (1 if transposed else 0,)), ((), ()))
    return lax.dot_general(left, right, dims, preferred_element_type=jnp.float32, precision=lax.Precision.HIGHEST)


def selector(me_ref, size, shifts):
    row = lax.broadcasted_iota(jnp.int32, (32, size), 0)
    index = lax.broadcasted_iota(jnp.int32, (32, size), 1)
    source = index // 64
    if shifts is not None:
        shift = source // 2
        for position, value in enumerate(shifts):
            shift = jnp.where(source // 2 == position, value, shift)
        source = (me_ref[0] // 2 + 4 - shift) % 4 * 2 + (me_ref[0] + source) % 2
    band = source * 2 + index // 16 % 2
    return jnp.where((row % 16 == band) & (row // 16 == index // 32 % 2), 1.0, 0.0)


def matched(total):
    row = lax.broadcasted_iota(jnp.int32, total.shape, 0)
    column = lax.broadcasted_iota(jnp.int32, total.shape, 1)
    return jnp.where(row % 16 == column % 16, total, 0.0)


def complex_lanes(table, first_lane):
    row = lax.broadcasted_iota(jnp.int32, (32, 128), 0)
    lane = lax.broadcasted_iota(jnp.int32, (32, 128), 1) - first_lane
    match = (lane >= 0) & (lane < 32) & (lane % 16 == row % 16)
    second, imag = lane // 16 == 1, row // 16 == 1
    with_real = jnp.where(match & (second == imag), 1.0, 0.0)
    with_imag = jnp.where(match & (second != imag), jnp.where(second, -1.0, 1.0), 0.0)
    return exact(table[:16], with_real, False) + exact(table[16:], with_imag, False)


def overlap_kernel(me_ref, *refs):
    *piece_refs, out_ref, total = refs
    step = pl.program_id(0)
    values = side_by_side(piece_refs)
    product = products_of(values, values)

    @pl.when(step == 0)
    def _():
        total[...] = product

    @pl.when(step == 1)
    def _():
        pick = selector(me_ref, 512, (0, 1, 2, 3))
        table = exact(exact(pick, matched(total[...] + product), False), pick, True)
        out_ref[...] = complex_lanes(table, 0)


def near_kernel(me_ref, left_ref, left_far_ref, kept_near, got_near, kept_far, got_far, out_ref, total):
    step = pl.program_id(0)
    product = products_of(left_ref[...].reshape(512, SLOTS), side_by_side([kept_near, got_near]))
    product += products_of(left_far_ref[...].reshape(512, SLOTS), side_by_side([kept_far, got_far]))

    @pl.when(step == 0)
    def _():
        total[...] = product

    @pl.when(step == 1)
    def _():
        pick = selector(me_ref, 512, None)
        table = exact(exact(pick, matched(total[...] + product), False), selector(me_ref, 128, (0,)), True)
        out_ref[...] = complex_lanes(table, 32)


def next_kernel(me_ref, left_ref, before_same, before_other, after_same, after_other, out_ref, total):
    step = pl.program_id(0)
    product = products_of(
        left_ref[...].reshape(512, SLOTS), side_by_side([before_same, before_other, after_same, after_other])
    )

    @pl.when(step == 0)
    def _():
        total[...] = product

    @pl.when(step == 1)
    def _():
        pick = selector(me_ref, 512, None)
        table = exact(exact(pick, matched(total[...] + product), False), selector(me_ref, 256, (1, 3)), True)
        out_ref[...] = complex_lanes(table, 32)


def gram_call(kernel, me, operands, shape, name):
    def spec(operand):
        _, size, block, start = operand
        return pl.BlockSpec((size, 1, 2, 2, 16, SLOTS), lambda g: (block, start + g, 0, 0, 0, 0))

    return pl.pallas_call(
        kernel,
        grid=(2,),
        in_specs=[pl.BlockSpec(memory_space=pltpu.SMEM)] + [spec(operand) for operand in operands],
        out_specs=pl.BlockSpec((16, 128), lambda g: (0, 0)),
        out_shape=jax.ShapeDtypeStruct((16, 128), jnp.float32),
        scratch_shapes=[pltpu.VMEM(shape, jnp.float32)],
        compiler_params=pltpu.CompilerParams(vmem_limit_bytes=60 * MIB),
        cost_estimate=pl.CostEstimate(flops=2_000_000_000, bytes_accessed=8_000_000, transcendentals=0),
        name=name,
    )(me, *[operand[0] for operand in operands])


def twofold_kernel(in_ref, out_ref):
    for half in range(2):
        out_ref[half, :, 0] = in_ref[half]
        out_ref[half, :, 1] = in_ref[1 - half]


def twofold_call(blocks):
    count = 2
    result = pl.pallas_call(
        twofold_kernel,
        grid=(4 // count,),
        in_specs=[pl.BlockSpec((2, count, 128, SLOTS), lambda i: (0, i, 0, 0))],
        out_specs=pl.BlockSpec((2, count, 2, 128, SLOTS), lambda i: (0, i, 0, 0, 0)),
        out_shape=jax.ShapeDtypeStruct((2, 4, 2, 128, SLOTS), jnp.bfloat16),
        compiler_params=pltpu.CompilerParams(vmem_limit_bytes=60 * MIB),
        cost_estimate=pl.CostEstimate(flops=0, bytes_accessed=12_000_000, transcendentals=0),
        name="twofold",
    )(blocks.reshape(2, 4, 128, SLOTS))
    return result.reshape(8, 256, SLOTS)


def summed(values, axis, steps, tied=None):
    size = lax.axis_size(axis)
    for step in steps:
        received = lax.ppermute(values, axis, [(i, i ^ step) for i in range(size)])
        if tied is not None:
            received, tied = lax.optimization_barrier((received, tied))
        values = values + received
    return values, tied


def moved(values, shift, other):
    return lax.ppermute(
        values, "band", [(i, (i // 2 + shift) % 4 * 2 + (i % 2 + other) % 2) for i in range(8)]
    )


def spread_blocks(kept, given, tied):
    chip = lax.axis_index("band") // 2
    got = moved(given, 0, 1)
    pairs = []
    for shift in range(4):
        target = (chip + shift) % 4
        pairs.append(
            jnp.concatenate(
                [lax.dynamic_slice_in_dim(kept, target, 1, 0), lax.dynamic_slice_in_dim(got, target, 1, 0)], axis=0
            )
        )
    tied, *pairs = lax.optimization_barrier((tied, *pairs))
    return [pairs[0]] + [moved(pairs[shift], shift, 0) for shift in (1, 2, 3)], tied


def plane_kernel(
    me_ref, place_ref, count_ref, upper_ref, wire_hbm, field_ref, forward_ref, backward_ref,
    out_hbm, kept_ref, given_ref, next_same, next_other, last_same, last_other, grid_ref, mid_ref, back_ref, side_ref, wire_ref, out_ref, stage_a, stage_b, stage_c, stage_d, list_ref, sems
):
    step = pl.program_id(0)
    lane = lax.broadcasted_iota(jnp.int32, (1, 128), 1)
    low = lane % 64 < 32
    sign = jnp.where(lane < 64, -1.0, 1.0).astype(jnp.bfloat16)

    def doubled(values):
        values = values.astype(jnp.bfloat16)
        return jnp.concatenate([values, pltpu.roll(values, 64, 1) * sign], axis=0)

    def exchange(first, second):
        return (
            jnp.where(low, first, pltpu.roll(second, 32, 1)),
            jnp.where(low, pltpu.roll(first, 96, 1), second),
        )

    @pl.when(step == 0)
    def _():
        fetch = pltpu.make_async_copy(wire_hbm, wire_ref, sems.at[0])
        fetch.start()

        def clear(i, carry):
            grid_ref[pl.ds(pl.multiple_of(i * 512, 512), 512), :] = jnp.zeros((512, 128), jnp.float32)
            return carry

        lax.fori_loop(0, ROWS // 512, clear, 0)
        grid_ref[pl.ds(ROWS, 8), :] = jnp.zeros((8, 128), jnp.float32)

        def group(p, total):
            def note(t, inner):
                list_ref[inner] = p * 15 + t
                return inner + 1

            return lax.fori_loop(0, count_ref[p], note, total)

        total = lax.fori_loop(0, GROUPS, group, 0)
        list_ref[total] = list_ref[total - 1]
        list_ref[total + 1] = list_ref[total - 1]
        for extra in range(2, 7):
            list_ref[total + extra] = list_ref[total - 1]
        list_ref[263] = (total + 1) // 2
        eye_row = lax.broadcasted_iota(jnp.int32, (128, 128), 0)
        eye_column = lax.broadcasted_iota(jnp.int32, (128, 128), 1)
        eye = jnp.where(eye_row == eye_column, 1.0, 0.0).astype(jnp.bfloat16)

        def rows_of(entry):
            p = entry // 15
            block = wire_ref[p, :, pl.ds(pl.multiple_of((entry - p * 15) * 128, 128), 128)]
            twice = jnp.concatenate([block[0:32], block[0:32], block[32:64], block[32:64]], axis=0)
            return lax.dot_general(eye, twice, (((1,), (1,)), ((), ())), preferred_element_type=jnp.float32)

        def spread(entry, stage):
            for u in range(128):
                grid_ref[pl.ds(place_ref[entry * 128 + u], 1), :] = stage[u : u + 1, :]

        def scatter(i, carry):
            entry = list_ref[2 * i]
            entry_b = list_ref[2 * i + 1]
            entry_c = list_ref[2 * i + 2]
            stage_b[...] = rows_of(entry_b)
            spread(entry, stage_a)
            stage_a[...] = rows_of(entry_c)
            spread(entry_b, stage_b)
            return carry

        fetch.wait()
        stage_a[...] = rows_of(list_ref[0])
        lax.fori_loop(0, list_ref[263], scatter, 0)

        def x_forward(i, carry):
            parts = []
            for j in range(N1):
                k = i * N1 + j
                first = grid_ref[pl.ds(pl.multiple_of(k * BOX, BOX), BOX), :]
                second = grid_ref[pl.ds(pl.multiple_of((k + HALF) * BOX, BOX), BOX), :]
                parts.append(doubled(jnp.where(low, first, second)))
            result = jnp.dot(forward_ref[...], jnp.concatenate(parts, axis=1), preferred_element_type=jnp.float32)
            for j in range(N1):
                k = i * N1 + j
                part = result[:, j * 128 : (j + 1) * 128]
                mid_ref[pl.ds(k, PAIRS, stride=PITCH), :] = part[:PAIRS]
                mid_ref[pl.ds(k + HALF, PAIRS, stride=PITCH), :] = part[PAIRS:]
            return carry

        lax.fori_loop(0, HALF // N1, x_forward, 0)

    def y_steps(i, carry):
        parts = []
        for j in range(N2):
            pair = step * PB + i * N2 + j
            base = pl.multiple_of(pair * PITCH, 8)
            first = mid_ref[pl.ds(base, HALF), :]
            second = mid_ref[pl.ds(base + HALF, HALF), :]
            even, odd = exchange(first, second)
            parts.append(doubled(jnp.concatenate([even, odd], axis=0)))
        spatial = jnp.dot(forward_ref[...], jnp.concatenate(parts, axis=1), preferred_element_type=jnp.float32)
        parts = []
        for j in range(N2):
            parts.append(doubled(spatial[:, j * 128 : (j + 1) * 128] * field_ref[i * N2 + j].astype(jnp.float32)))
        result = jnp.dot(backward_ref[...], jnp.concatenate(parts, axis=1), preferred_element_type=jnp.float32)
        for j in range(N2):
            pair = step * PB + i * N2 + j
            back_ref[pl.ds(pair, BOX, stride=PITCHB), :] = result[:, j * 128 : (j + 1) * 128]
        return carry

    lax.fori_loop(0, PB // N2, y_steps, 0)

    @pl.when(step == pl.num_programs(0) - 1)
    def _():
        def x_backward(i, carry):
            parts = []
            for j in range(N4):
                k = i * N4 + j
                first = back_ref[pl.ds(pl.multiple_of(k * PITCHB, 8), PAIRS), :]
                second = back_ref[pl.ds(pl.multiple_of((k + HALF) * PITCHB, 8), PAIRS), :]
                even, odd = exchange(first, second)
                parts.append(doubled(jnp.concatenate([even, odd], axis=0)))
            result = jnp.dot(backward_ref[...], jnp.concatenate(parts, axis=1), preferred_element_type=jnp.float32)
            for j in range(N4):
                k = i * N4 + j
                part = result[:, j * 128 : (j + 1) * 128]
                grid_ref[pl.ds(pl.multiple_of(k * BOX, BOX), BOX), :] = part
                grid_ref[pl.ds(pl.multiple_of((k + HALF) * BOX, BOX), BOX), :] = part
            return carry

        lax.fori_loop(0, HALF // N4, x_backward, 0)
        select_row = lax.broadcasted_iota(jnp.int32, (128, 128), 0)
        select_column = lax.broadcasted_iota(jnp.int32, (128, 128), 1)
        source = select_row % 64 // 32 * 64 + select_row // 64 * 32 + select_row % 32
        select = jnp.where(select_column == source, 1.0, 0.0).astype(jnp.bfloat16)
        origin = pl.multiple_of((step - (pl.num_programs(0) - 1)) * 8, 8)

        def side_of(p):
            return (p // 2 + me_ref[0]) % 2

        def write_two(entry, entry_b, stage):
            both = lax.dot_general(
                select, stage[...].astype(jnp.bfloat16), (((1,), (1,)), ((), ())), preferred_element_type=jnp.float32
            )
            for n, e in enumerate((entry, entry_b)):
                p = e // 15
                base = pl.multiple_of((e - p * 15) * 128, 128)
                upper = upper_ref[pl.ds(e, 1), :] > 0.0
                part = both[:, n * 128 : (n + 1) * 128]
                values = jnp.where(upper, part[64:], part[:64]).astype(jnp.bfloat16)
                out_ref[p, :, pl.ds(base, 128)] = values
                side_ref[side_of(p), p // 4, p % 2, :, pl.ds(base, 128)] = values

        def gather_two(entry, entry_b, stage):
            for n, e in enumerate((entry, entry_b)):
                for u in range(128):
                    stage[pl.ds(origin + n * 128 + u, 1), :] = grid_ref[pl.ds(place_ref[e * 128 + u], 1), :]

        def pick_four(i, carry):
            e = [list_ref[4 * i + n] for n in range(6)]
            gather_two(e[2], e[3], stage_d)
            write_two(e[0], e[1], stage_c)
            gather_two(e[4], e[5], stage_c)
            write_two(e[2], e[3], stage_d)
            return carry

        def group(p, carry):
            def blank(t, inner):
                base = pl.multiple_of(t * 128, 128)
                blank = jnp.zeros((64, 128), jnp.bfloat16)
                out_ref[p, :, pl.ds(base, 128)] = blank
                side_ref[side_of(p), p // 4, p % 2, :, pl.ds(base, 128)] = blank
                return inner

            return lax.fori_loop(count_ref[p], SLOTS // 128, blank, carry)

        lax.fori_loop(0, GROUPS, group, 0)
        gather_two(list_ref[0], list_ref[1], stage_c)
        lax.fori_loop(0, (list_ref[263] + 1) // 2, pick_four, 0)
        chip = me_ref[0] // 2
        after, far, before = (chip + 1) % 4, (chip + 2) % 4, (chip + 3) % 4
        routes = [
            (side_ref.at[0, after], next_same),
            (side_ref.at[1, after], next_other),
            (side_ref.at[0, before], last_same),
            (side_ref.at[1, before], last_other),
            (side_ref.at[1, chip], given_ref.at[0]),
            (side_ref.at[1, far], given_ref.at[1]),
            (side_ref.at[0, chip], kept_ref.at[0]),
            (side_ref.at[0, far], kept_ref.at[1]),
        ]
        routes.append((out_ref, out_hbm))
        copies = [pltpu.make_async_copy(*route, sems.at[1 + n]) for n, route in enumerate(routes)]
        for copy in copies:
            copy.start()
        for copy in copies:
            copy.wait()


def plane_call(me, place, count, upper, wire, field, forward, backward):
    whole = lambda shape: pl.BlockSpec(shape, lambda i: (0,) * len(shape), pipeline_mode=pl.Buffered(1))
    return pl.pallas_call(
        plane_kernel,
        grid=(PAIRS // PB,),
        in_specs=[
            pl.BlockSpec(memory_space=pltpu.SMEM),
            pl.BlockSpec(memory_space=pltpu.SMEM),
            pl.BlockSpec(memory_space=pltpu.SMEM),
            whole((GROUPS * SLOTS // 128, 128)),
            pl.BlockSpec(memory_space=pl.ANY),
            pl.BlockSpec((PB, GRID, 128), lambda i: (i, 0, 0)),
            whole((GRID, 2 * BOX)),
            whole((BOX, 2 * GRID)),
        ],
        out_specs=[pl.BlockSpec(memory_space=pl.ANY)] * 7,
        out_shape=[jax.ShapeDtypeStruct((GROUPS, 64, SLOTS), jnp.bfloat16)]
        + [jax.ShapeDtypeStruct((2, 2, 64, SLOTS), jnp.bfloat16)] * 2
        + [jax.ShapeDtypeStruct((2, 64, SLOTS), jnp.bfloat16)] * 4,
        scratch_shapes=[
            pltpu.VMEM((ROWS + 8, 128), jnp.float32),
            pltpu.VMEM((PAIRS * PITCH, 128), jnp.float32),
            pltpu.VMEM((BOX * PITCHB, 128), jnp.float32),
            pltpu.VMEM((2, 4, 2, 64, SLOTS), jnp.bfloat16),
            pltpu.VMEM((GROUPS, 64, SLOTS), jnp.bfloat16),
            pltpu.VMEM((GROUPS, 64, SLOTS), jnp.bfloat16),
            pltpu.VMEM((128, 128), jnp.float32),
            pltpu.VMEM((128, 128), jnp.float32),
            pltpu.VMEM((256, 128), jnp.float32),
            pltpu.VMEM((256, 128), jnp.float32),
            pltpu.SMEM((264,), jnp.int32),
            pltpu.SemaphoreType.DMA((10,)),
        ],
        compiler_params=pltpu.CompilerParams(vmem_limit_bytes=62 * MIB),
        cost_estimate=pl.CostEstimate(flops=13_000_000_000, bytes_accessed=24_000_000, transcendentals=0),
        name="planes",
    )(me, place, count, upper, wire, field, forward, backward)


def field_kernel(lower_ref, upper_ref, out_ref):
    blank = jnp.zeros((1, lower_ref.shape[-1]), jnp.float32)
    lower = jnp.concatenate([lower_ref[...], blank], axis=0).astype(jnp.bfloat16)
    upper = jnp.concatenate([upper_ref[...], blank], axis=0).astype(jnp.bfloat16)
    once = jnp.concatenate([lower, lower, upper, upper], axis=0)
    out_ref[...] = jnp.concatenate([once, once], axis=0).T.reshape(PB, GRID, 128)


def field_call(potential):
    lanes = PB * GRID
    return pl.pallas_call(
        field_kernel,
        grid=(PAIRS // PB,),
        in_specs=[
            pl.BlockSpec((PLANES, lanes), lambda i: (0, i)),
            pl.BlockSpec((PLANES, lanes), lambda i: (0, i + PAIRS // PB)),
        ],
        out_specs=pl.BlockSpec((PB, GRID, 128), lambda i: (i, 0, 0)),
        out_shape=jax.ShapeDtypeStruct((PAIRS, GRID, 128), jnp.bfloat16),
        compiler_params=pltpu.CompilerParams(vmem_limit_bytes=60 * MIB),
        cost_estimate=pl.CostEstimate(flops=0, bytes_accessed=18_000_000, transcendentals=0),
        name="field",
    )(potential, potential)


def local(orbitals, potential, stick_column, column_slot):
    z_forward, z_backward, forward, backward = (jnp.asarray(table) for table in tables())
    live_all = stick_column >= 0
    own = lax.dynamic_slice_in_dim(stick_column, lax.axis_index("fft") * SLOTS, SLOTS)
    live = (own >= 0).astype(jnp.float32)[None, :]
    column_x, column_y = stick_column // GRID, stick_column % GRID
    box_x = jnp.where(column_x < GRID // 2, column_x + HALF, column_x - (GRID - HALF))
    box_y = jnp.where(column_y < GRID // 2, column_y + HALF, column_y - (GRID - HALF))
    place = jnp.where(live_all, box_y * BOX + box_x, ROWS)
    count = (jnp.sum(live_all.reshape(GROUPS, SLOTS).astype(jnp.int32), axis=1) + 127) // 128
    upper = (live_all & (box_y >= HALF)).astype(jnp.float32).reshape(GROUPS * SLOTS // 128, 128)
    me = lax.axis_index("band").astype(jnp.int32)[None]
    core = me % 2

    wire, kept, given = z_forward_call(core, orbitals.transpose(0, 2, 1), live, z_forward)
    incoming = lax.all_to_all(wire.reshape(GROUPS, 64, SLOTS), "fft", split_axis=0, concat_axis=0, tiled=True)
    shares, potential = spread_blocks(kept, given, potential)
    field = field_call(potential)
    incoming, field, place, count, upper, *shares = lax.optimization_barrier(
        (incoming, field, place, count, upper, *shares)
    )
    left = lax.all_to_all(twofold_call(incoming), "band", split_axis=0, concat_axis=0, tiled=True)
    left = left.reshape(8, 4, 2, 2, 16, SLOTS)
    outgoing, kept, given, *sides = plane_call(me, place, count, upper, incoming, field, forward, backward)
    piece = (1, 2, 2, 2, 16, SLOTS)
    sides = [side.reshape(piece) for side in sides]
    arrived = [moved(side, shift, other) for side, (shift, other) in zip(sides, ((1, 0), (1, 1), (3, 0), (3, 1)))]
    kept, got = kept.reshape(2, 2, 2, 2, 16, SLOTS), moved(given.reshape(2, 2, 2, 2, 16, SLOTS), 0, 1)
    returned = lax.all_to_all(outgoing, "fft", split_axis=0, concat_axis=0, tiled=True)
    products = gram_call(overlap_kernel, me, [(share, 2, 0, 0) for share in shares], (512, 512), "overlap")
    lefts = [(left, 8, 0, 0), (left, 8, 0, 2)]
    nears = [(kept, 1, 0, 0), (got, 1, 0, 0), (kept, 1, 1, 0), (got, 1, 1, 0)]
    products += gram_call(near_kernel, me, lefts + nears, (512, 128), "near")
    products += gram_call(next_kernel, me, lefts[:1] + [(side, 1, 0, 0) for side in arrived], (512, 256), "next")
    applied = z_backward_call(returned.reshape(GROUPS, 2, 2, ZPAD, SLOTS), live, z_backward)
    products, _ = summed(products, "band", (1, 2, 4))
    products, _ = summed(products, "fft", (1, 2))
    products, applied = summed(products, "fft", (4,), applied)
    products, _ = summed(products, "fft", (8,))
    products = products * (1.0 / (2.0 * STICKS * GRID))
    products = products[:, :64].reshape(16, 4, 16).transpose(1, 0, 2)
    return (applied.transpose(0, 2, 1), products[0:2], products[2:4])


def solution(mesh):
    return jax.shard_map(
        local,
        mesh=mesh,
        in_specs=(P("band", "fft", None), P("fft", None), P(), P()),
        out_specs=(P("band", "fft", None), P(), P()),
        check_vma=False,
    )
```

```python
import functools
import math

import jax
import jax.numpy as jnp
import ml_dtypes
import numpy as np
from jax import lax
from jax.experimental import pallas as pl
from jax.experimental.pallas import tpu as pltpu
from jax.sharding import PartitionSpec as P

STICKS = 24576
GRID = 240
SLOTS = 1920
GROUPS = 16
PLANES = 15
ZPAD = 16
BOX = 192
HALF = BOX // 2
PAIRS = GRID // 2
ROWS = BOX * BOX
PITCH = 200
PITCHB = 120
PB = 24
N1 = 12
N2 = 12
N4 = 12
MIB = 1 << 20


def trig():
    counter = np.arange(GRID, dtype=np.int32)
    phases = counter[:, None] * counter[None, :] % GRID
    angles = phases.astype(np.float32) * np.float32(2.0 * math.pi / GRID)
    factor = np.float32(1.0 / math.sqrt(GRID))
    cosine = (np.cos(angles) * factor).astype(ml_dtypes.bfloat16)
    sine = (np.sin(angles) * factor).astype(ml_dtypes.bfloat16)
    return cosine, sine


def tables():
    cosine, sine = trig()
    box = np.arange(BOX) - HALF
    box = np.where(box < 0, box + GRID, box)
    z_forward = np.zeros((GROUPS, 2, ZPAD, 2, GRID), ml_dtypes.bfloat16)
    cos_z = cosine.reshape(GROUPS, PLANES, GRID)
    sin_z = sine.reshape(GROUPS, PLANES, GRID)
    z_forward[:, 0, :PLANES, 0] = cos_z
    z_forward[:, 0, :PLANES, 1] = -sin_z
    z_forward[:, 1, :PLANES, 0] = sin_z
    z_forward[:, 1, :PLANES, 1] = cos_z
    z_forward = z_forward.reshape(GROUPS * 2 * ZPAD, 2 * GRID)
    z_backward = np.ascontiguousarray(z_forward.T)
    cos_box, sin_box = cosine[:, box], sine[:, box]
    forward = np.concatenate([cos_box, sin_box], axis=1)
    backward = np.concatenate([cos_box.T, -sin_box.T], axis=1)
    return z_forward, z_backward, forward, backward


def z_forward_kernel(core_ref, orbit_ref, live_ref, table_ref, wire_ref, kept_ref, given_ref, masked_ref):
    masked_ref[...] = (orbit_ref[0].astype(jnp.float32) * live_ref[...]).astype(jnp.bfloat16)
    for core in range(2):

        @pl.when(core_ref[0] == core)
        def _():
            for q in range(15):
                target = kept_ref if q // 2 % 2 == core else given_ref
                for c in range(2):
                    start = c * GRID + q * 16
                    target[q // 4, q % 2, c, 0] = masked_ref[start : start + 16]
            target = kept_ref if core == 1 else given_ref
            for c in range(2):
                target[3, 1, c, 0] = jnp.zeros((16, SLOTS), jnp.bfloat16)

    values = jnp.dot(table_ref[...], masked_ref[...], preferred_element_type=jnp.float32).astype(jnp.bfloat16)
    wire_ref[...] = values.reshape(GROUPS, 2, 1, ZPAD, SLOTS)


def z_forward_call(core, orbits, live, table):
    share = pl.BlockSpec((4, 2, 2, 1, 16, SLOTS), lambda b: (0, 0, 0, b, 0, 0))
    return pl.pallas_call(
        z_forward_kernel,
        grid=(2,),
        in_specs=[
            pl.BlockSpec(memory_space=pltpu.SMEM),
            pl.BlockSpec((1, 2 * GRID, SLOTS), lambda b: (b, 0, 0)),
            pl.BlockSpec((1, SLOTS), lambda b: (0, 0)),
            pl.BlockSpec((512, 2 * GRID), lambda b: (0, 0)),
        ],
        out_specs=[pl.BlockSpec((GROUPS, 2, 1, ZPAD, SLOTS), lambda b: (0, 0, b, 0, 0)), share, share],
        out_shape=[jax.ShapeDtypeStruct((GROUPS, 2, 2, ZPAD, SLOTS), jnp.bfloat16)]
        + [jax.ShapeDtypeStruct((4, 2, 2, 2, 16, SLOTS), jnp.bfloat16)] * 2,
        scratch_shapes=[pltpu.VMEM((2 * GRID, SLOTS), jnp.bfloat16)],
        compiler_params=pltpu.CompilerParams(vmem_limit_bytes=60 * MIB),
        cost_estimate=pl.CostEstimate(flops=1_800_000_000, bytes_accessed=12_000_000, transcendentals=0),
        name="z_forward",
    )(core, orbits, live, table)


def z_backward_kernel(wire_ref, live_ref, table_ref, out_ref):
    values = wire_ref[...].reshape(512, SLOTS)
    applied = jnp.dot(table_ref[...], values, preferred_element_type=jnp.float32)
    out_ref[0] = (applied * live_ref[...]).astype(jnp.bfloat16)


def z_backward_call(wire, live, table):
    return pl.pallas_call(
        z_backward_kernel,
        grid=(2,),
        in_specs=[
            pl.BlockSpec((GROUPS, 2, 1, ZPAD, SLOTS), lambda b: (0, 0, b, 0, 0)),
            pl.BlockSpec((1, SLOTS), lambda b: (0, 0)),
            pl.BlockSpec((2 * GRID, 512), lambda b: (0, 0)),
        ],
        out_specs=pl.BlockSpec((1, 2 * GRID, SLOTS), lambda b: (b, 0, 0)),
        out_shape=jax.ShapeDtypeStruct((2, 2 * GRID, SLOTS), jnp.bfloat16),
        compiler_params=pltpu.CompilerParams(vmem_limit_bytes=60 * MIB),
        cost_estimate=pl.CostEstimate(flops=1_800_000_000, bytes_accessed=8_000_000, transcendentals=0),
        name="z_backward",
    )(wire, live, table)


def side_by_side(refs):
    return jnp.concatenate([ref[...].reshape(-1, SLOTS) for ref in refs], axis=0)


def products_of(left, right):
    return lax.dot_general(left, right, (((1,), (1,)), ((), ())), preferred_element_type=jnp.float32)


def exact(left, right, transposed):
    dims = (((1,), (1 if transposed else 0,)), ((), ()))
    return lax.dot_general(left, right, dims, preferred_element_type=jnp.float32, precision=lax.Precision.HIGHEST)


def selector(me_ref, size, shifts):
    row = lax.broadcasted_iota(jnp.int32, (32, size), 0)
    index = lax.broadcasted_iota(jnp.int32, (32, size), 1)
    source = index // 64
    if shifts is not None:
        shift = source // 2
        for position, value in enumerate(shifts):
            shift = jnp.where(source // 2 == position, value, shift)
        source = (me_ref[0] // 2 + 4 - shift) % 4 * 2 + (me_ref[0] + source) % 2
    band = source * 2 + index // 16 % 2
    return jnp.where((row % 16 == band) & (row // 16 == index // 32 % 2), 1.0, 0.0)


def matched(total):
    row = lax.broadcasted_iota(jnp.int32, total.shape, 0)
    column = lax.broadcasted_iota(jnp.int32, total.shape, 1)
    return jnp.where(row % 16 == column % 16, total, 0.0)


def complex_lanes(table, first_lane):
    row = lax.broadcasted_iota(jnp.int32, (32, 128), 0)
    lane = lax.broadcasted_iota(jnp.int32, (32, 128), 1) - first_lane
    match = (lane >= 0) & (lane < 32) & (lane % 16 == row % 16)
    second, imag = lane // 16 == 1, row // 16 == 1
    with_real = jnp.where(match & (second == imag), 1.0, 0.0)
    with_imag = jnp.where(match & (second != imag), jnp.where(second, -1.0, 1.0), 0.0)
    return exact(table[:16], with_real, False) + exact(table[16:], with_imag, False)


def overlap_kernel(me_ref, *refs):
    *piece_refs, out_ref, total = refs
    step = pl.program_id(0)
    values = side_by_side(piece_refs)
    product = products_of(values, values)

    @pl.when(step == 0)
    def _():
        total[...] = product

    @pl.when(step == 1)
    def _():
        pick = selector(me_ref, 512, (0, 1, 2, 3))
        table = exact(exact(pick, matched(total[...] + product), False), pick, True)
        out_ref[...] = complex_lanes(table, 0)


def near_kernel(me_ref, left_ref, left_far_ref, kept_near, got_near, kept_far, got_far, out_ref, total):
    step = pl.program_id(0)
    product = products_of(left_ref[...].reshape(512, SLOTS), side_by_side([kept_near, got_near]))
    product += products_of(left_far_ref[...].reshape(512, SLOTS), side_by_side([kept_far, got_far]))

    @pl.when(step == 0)
    def _():
        total[...] = product

    @pl.when(step == 1)
    def _():
        pick = selector(me_ref, 512, None)
        table = exact(exact(pick, matched(total[...] + product), False), selector(me_ref, 128, (0,)), True)
        out_ref[...] = complex_lanes(table, 32)


def next_kernel(me_ref, left_ref, before_same, before_other, after_same, after_other, out_ref, total):
    step = pl.program_id(0)
    product = products_of(
        left_ref[...].reshape(512, SLOTS), side_by_side([before_same, before_other, after_same, after_other])
    )

    @pl.when(step == 0)
    def _():
        total[...] = product

    @pl.when(step == 1)
    def _():
        pick = selector(me_ref, 512, None)
        table = exact(exact(pick, matched(total[...] + product), False), selector(me_ref, 256, (1, 3)), True)
        out_ref[...] = complex_lanes(table, 32)


def gram_call(kernel, me, operands, shape, name):
    def spec(operand):
        _, size, block, start = operand
        return pl.BlockSpec((size, 1, 2, 2, 16, SLOTS), lambda g: (block, start + g, 0, 0, 0, 0))

    return pl.pallas_call(
        kernel,
        grid=(2,),
        in_specs=[pl.BlockSpec(memory_space=pltpu.SMEM)] + [spec(operand) for operand in operands],
        out_specs=pl.BlockSpec((16, 128), lambda g: (0, 0)),
        out_shape=jax.ShapeDtypeStruct((16, 128), jnp.float32),
        scratch_shapes=[pltpu.VMEM(shape, jnp.float32)],
        compiler_params=pltpu.CompilerParams(vmem_limit_bytes=60 * MIB),
        cost_estimate=pl.CostEstimate(flops=2_000_000_000, bytes_accessed=8_000_000, transcendentals=0),
        name=name,
    )(me, *[operand[0] for operand in operands])


def twofold_kernel(in_ref, out_ref, held, in_sems, out_sems):
    loads = [pltpu.make_async_copy(in_ref.at[d], held.at[d], in_sems.at[d]) for d in range(8)]
    for load in loads:
        load.start()
    stores = []
    for d in range(8):
        loads[d].wait()
        for half, target in enumerate((d, (d + 4) % 8)):
            store = pltpu.make_async_copy(held.at[d], out_ref.at[target, half], out_sems.at[2 * d + half])
            store.start()
            stores.append(store)
    for store in stores:
        store.wait()


def twofold_call(blocks):
    result = pl.pallas_call(
        twofold_kernel,
        in_specs=[pl.BlockSpec(memory_space=pl.ANY)],
        out_specs=pl.BlockSpec(memory_space=pl.ANY),
        out_shape=jax.ShapeDtypeStruct((8, 2, 128, SLOTS), jnp.bfloat16),
        scratch_shapes=[
            pltpu.VMEM((8, 128, SLOTS), jnp.bfloat16),
            pltpu.SemaphoreType.DMA((8,)),
            pltpu.SemaphoreType.DMA((16,)),
        ],
        compiler_params=pltpu.CompilerParams(vmem_limit_bytes=60 * MIB),
        cost_estimate=pl.CostEstimate(flops=0, bytes_accessed=12_000_000, transcendentals=0),
        name="twofold",
    )(blocks.reshape(8, 128, SLOTS))
    return result.reshape(8, 256, SLOTS)


def summed(values, axis, steps, tied=None):
    size = lax.axis_size(axis)
    for step in steps:
        received = lax.ppermute(values, axis, [(i, i ^ step) for i in range(size)])
        if tied is not None:
            received, tied = lax.optimization_barrier((received, tied))
        values = values + received
    return values, tied


def moved(values, shift, other):
    return lax.ppermute(
        values, "band", [(i, (i // 2 + shift) % 4 * 2 + (i % 2 + other) % 2) for i in range(8)]
    )


def spread_blocks(kept, given, tied):
    chip = lax.axis_index("band") // 2
    got = moved(given, 0, 1)
    pairs = []
    for shift in range(4):
        target = (chip + shift) % 4
        pairs.append(
            jnp.concatenate(
                [lax.dynamic_slice_in_dim(kept, target, 1, 0), lax.dynamic_slice_in_dim(got, target, 1, 0)], axis=0
            )
        )
    tied, *pairs = lax.optimization_barrier((tied, *pairs))
    return [pairs[0]] + [moved(pairs[shift], shift, 0) for shift in (1, 2, 3)], tied


def plane_kernel(
    me_ref, place_ref, count_ref, upper_ref, wire_hbm, field_ref, forward_ref, backward_ref,
    out_hbm, kept_ref, given_ref, next_same, next_other, last_same, last_other, grid_ref, mid_ref, back_ref, side_ref, wire_ref, out_ref, stage_a, stage_b, stage_c, stage_d, list_ref, sems
):
    step = pl.program_id(0)
    lane = lax.broadcasted_iota(jnp.int32, (1, 128), 1)
    low = lane % 64 < 32
    sign = jnp.where(lane < 64, -1.0, 1.0).astype(jnp.bfloat16)

    def doubled(values):
        values = values.astype(jnp.bfloat16)
        return jnp.concatenate([values, pltpu.roll(values, 64, 1) * sign], axis=0)

    def exchange(first, second):
        return (
            jnp.where(low, first, pltpu.roll(second, 32, 1)),
            jnp.where(low, pltpu.roll(first, 96, 1), second),
        )

    @pl.when(step == 0)
    def _():
        fetch = pltpu.make_async_copy(wire_hbm, wire_ref, sems.at[0])
        fetch.start()

        def clear(i, carry):
            grid_ref[pl.ds(pl.multiple_of(i * 512, 512), 512), :] = jnp.zeros((512, 128), jnp.float32)
            return carry

        lax.fori_loop(0, ROWS // 512, clear, 0)
        grid_ref[pl.ds(ROWS, 8), :] = jnp.zeros((8, 128), jnp.float32)

        def group(p, total):
            def note(t, inner):
                list_ref[inner] = p * 15 + t
                return inner + 1

            return lax.fori_loop(0, count_ref[p], note, total)

        total = lax.fori_loop(0, GROUPS, group, 0)
        list_ref[total] = list_ref[total - 1]
        list_ref[total + 1] = list_ref[total - 1]
        for extra in range(2, 7):
            list_ref[total + extra] = list_ref[total - 1]
        list_ref[263] = (total + 1) // 2
        eye_row = lax.broadcasted_iota(jnp.int32, (128, 128), 0)
        eye_column = lax.broadcasted_iota(jnp.int32, (128, 128), 1)
        eye = jnp.where(eye_row == eye_column, 1.0, 0.0).astype(jnp.bfloat16)

        def rows_of(entry):
            p = entry // 15
            block = wire_ref[p, :, pl.ds(pl.multiple_of((entry - p * 15) * 128, 128), 128)]
            twice = jnp.concatenate([block[0:32], block[0:32], block[32:64], block[32:64]], axis=0)
            return lax.dot_general(eye, twice, (((1,), (1,)), ((), ())), preferred_element_type=jnp.float32)

        def spread(entry, stage):
            for u in range(128):
                grid_ref[pl.ds(place_ref[entry * 128 + u], 1), :] = stage[u : u + 1, :]

        def scatter(i, carry):
            entry = list_ref[2 * i]
            entry_b = list_ref[2 * i + 1]
            entry_c = list_ref[2 * i + 2]
            stage_b[...] = rows_of(entry_b)
            spread(entry, stage_a)
            stage_a[...] = rows_of(entry_c)
            spread(entry_b, stage_b)
            return carry

        fetch.wait()
        stage_a[...] = rows_of(list_ref[0])
        lax.fori_loop(0, list_ref[263], scatter, 0)

        def x_forward(i, carry):
            parts = []
            for j in range(N1):
                k = i * N1 + j
                first = grid_ref[pl.ds(pl.multiple_of(k * BOX, BOX), BOX), :]
                second = grid_ref[pl.ds(pl.multiple_of((k + HALF) * BOX, BOX), BOX), :]
                parts.append(doubled(jnp.where(low, first, second)))
            result = jnp.dot(forward_ref[...], jnp.concatenate(parts, axis=1), preferred_element_type=jnp.float32)
            for j in range(N1):
                k = i * N1 + j
                part = result[:, j * 128 : (j + 1) * 128]
                mid_ref[pl.ds(k, PAIRS, stride=PITCH), :] = part[:PAIRS]
                mid_ref[pl.ds(k + HALF, PAIRS, stride=PITCH), :] = part[PAIRS:]
            return carry

        lax.fori_loop(0, HALF // N1, x_forward, 0)

    def y_steps(i, carry):
        parts = []
        for j in range(N2):
            pair = step * PB + i * N2 + j
            base = pl.multiple_of(pair * PITCH, 8)
            first = mid_ref[pl.ds(base, HALF), :]
            second = mid_ref[pl.ds(base + HALF, HALF), :]
            even, odd = exchange(first, second)
            parts.append(doubled(jnp.concatenate([even, odd], axis=0)))
        spatial = jnp.dot(forward_ref[...], jnp.concatenate(parts, axis=1), preferred_element_type=jnp.float32)
        parts = []
        for j in range(N2):
            parts.append(doubled(spatial[:, j * 128 : (j + 1) * 128] * field_ref[i * N2 + j].astype(jnp.float32)))
        result = jnp.dot(backward_ref[...], jnp.concatenate(parts, axis=1), preferred_element_type=jnp.float32)
        for j in range(N2):
            pair = step * PB + i * N2 + j
            back_ref[pl.ds(pair, BOX, stride=PITCHB), :] = result[:, j * 128 : (j + 1) * 128]
        return carry

    lax.fori_loop(0, PB // N2, y_steps, 0)

    @pl.when(step == pl.num_programs(0) - 1)
    def _():
        def x_backward(i, carry):
            parts = []
            for j in range(N4):
                k = i * N4 + j
                first = back_ref[pl.ds(pl.multiple_of(k * PITCHB, 8), PAIRS), :]
                second = back_ref[pl.ds(pl.multiple_of((k + HALF) * PITCHB, 8), PAIRS), :]
                even, odd = exchange(first, second)
                parts.append(doubled(jnp.concatenate([even, odd], axis=0)))
            result = jnp.dot(backward_ref[...], jnp.concatenate(parts, axis=1), preferred_element_type=jnp.float32)
            for j in range(N4):
                k = i * N4 + j
                part = result[:, j * 128 : (j + 1) * 128]
                grid_ref[pl.ds(pl.multiple_of(k * BOX, BOX), BOX), :] = part
                grid_ref[pl.ds(pl.multiple_of((k + HALF) * BOX, BOX), BOX), :] = part
            return carry

        lax.fori_loop(0, HALF // N4, x_backward, 0)
        select_row = lax.broadcasted_iota(jnp.int32, (128, 128), 0)
        select_column = lax.broadcasted_iota(jnp.int32, (128, 128), 1)
        source = select_row % 64 // 32 * 64 + select_row // 64 * 32 + select_row % 32
        select = jnp.where(select_column == source, 1.0, 0.0).astype(jnp.bfloat16)
        origin = pl.multiple_of((step - (pl.num_programs(0) - 1)) * 8, 8)

        def side_of(p):
            return (p // 2 + me_ref[0]) % 2

        def write_two(entry, entry_b, stage):
            both = lax.dot_general(
                select, stage[...].astype(jnp.bfloat16), (((1,), (1,)), ((), ())), preferred_element_type=jnp.float32
            )
            for n, e in enumerate((entry, entry_b)):
                p = e // 15
                base = pl.multiple_of((e - p * 15) * 128, 128)
                upper = upper_ref[pl.ds(e, 1), :] > 0.0
                part = both[:, n * 128 : (n + 1) * 128]
                values = jnp.where(upper, part[64:], part[:64]).astype(jnp.bfloat16)
                out_ref[p, :, pl.ds(base, 128)] = values
                side_ref[side_of(p), p // 4, p % 2, :, pl.ds(base, 128)] = values

        def gather_two(entry, entry_b, stage):
            for n, e in enumerate((entry, entry_b)):
                for u in range(128):
                    stage[pl.ds(origin + n * 128 + u, 1), :] = grid_ref[pl.ds(place_ref[e * 128 + u], 1), :]

        def pick_four(i, carry):
            e = [list_ref[4 * i + n] for n in range(6)]
            gather_two(e[2], e[3], stage_d)
            write_two(e[0], e[1], stage_c)
            gather_two(e[4], e[5], stage_c)
            write_two(e[2], e[3], stage_d)
            return carry

        def group(p, carry):
            def blank(t, inner):
                base = pl.multiple_of(t * 128, 128)
                blank = jnp.zeros((64, 128), jnp.bfloat16)
                out_ref[p, :, pl.ds(base, 128)] = blank
                side_ref[side_of(p), p // 4, p % 2, :, pl.ds(base, 128)] = blank
                return inner

            return lax.fori_loop(count_ref[p], SLOTS // 128, blank, carry)

        lax.fori_loop(0, GROUPS, group, 0)
        gather_two(list_ref[0], list_ref[1], stage_c)
        lax.fori_loop(0, (list_ref[263] + 1) // 2, pick_four, 0)
        chip = me_ref[0] // 2
        after, far, before = (chip + 1) % 4, (chip + 2) % 4, (chip + 3) % 4
        routes = [
            (side_ref.at[0, after], next_same),
            (side_ref.at[1, after], next_other),
            (side_ref.at[0, before], last_same),
            (side_ref.at[1, before], last_other),
            (side_ref.at[1, chip], given_ref.at[0]),
            (side_ref.at[1, far], given_ref.at[1]),
            (side_ref.at[0, chip], kept_ref.at[0]),
            (side_ref.at[0, far], kept_ref.at[1]),
        ]
        routes.append((out_ref, out_hbm))
        copies = [pltpu.make_async_copy(*route, sems.at[1 + n]) for n, route in enumerate(routes)]
        for copy in copies:
            copy.start()
        for copy in copies:
            copy.wait()


def plane_call(me, place, count, upper, wire, field, forward, backward):
    whole = lambda shape: pl.BlockSpec(shape, lambda i: (0,) * len(shape), pipeline_mode=pl.Buffered(1))
    return pl.pallas_call(
        plane_kernel,
        grid=(PAIRS // PB,),
        in_specs=[
            pl.BlockSpec(memory_space=pltpu.SMEM),
            pl.BlockSpec(memory_space=pltpu.SMEM),
            pl.BlockSpec(memory_space=pltpu.SMEM),
            whole((GROUPS * SLOTS // 128, 128)),
            pl.BlockSpec(memory_space=pl.ANY),
            pl.BlockSpec((PB, GRID, 128), lambda i: (i, 0, 0)),
            whole((GRID, 2 * BOX)),
            whole((BOX, 2 * GRID)),
        ],
        out_specs=[pl.BlockSpec(memory_space=pl.ANY)] * 7,
        out_shape=[jax.ShapeDtypeStruct((GROUPS, 64, SLOTS), jnp.bfloat16)]
        + [jax.ShapeDtypeStruct((2, 2, 64, SLOTS), jnp.bfloat16)] * 2
        + [jax.ShapeDtypeStruct((2, 64, SLOTS), jnp.bfloat16)] * 4,
        scratch_shapes=[
            pltpu.VMEM((ROWS + 8, 128), jnp.float32),
            pltpu.VMEM((PAIRS * PITCH, 128), jnp.float32),
            pltpu.VMEM((BOX * PITCHB, 128), jnp.float32),
            pltpu.VMEM((2, 4, 2, 64, SLOTS), jnp.bfloat16),
            pltpu.VMEM((GROUPS, 64, SLOTS), jnp.bfloat16),
            pltpu.VMEM((GROUPS, 64, SLOTS), jnp.bfloat16),
            pltpu.VMEM((128, 128), jnp.float32),
            pltpu.VMEM((128, 128), jnp.float32),
            pltpu.VMEM((256, 128), jnp.float32),
            pltpu.VMEM((256, 128), jnp.float32),
            pltpu.SMEM((264,), jnp.int32),
            pltpu.SemaphoreType.DMA((10,)),
        ],
        compiler_params=pltpu.CompilerParams(vmem_limit_bytes=62 * MIB),
        cost_estimate=pl.CostEstimate(flops=13_000_000_000, bytes_accessed=24_000_000, transcendentals=0),
        name="planes",
    )(me, place, count, upper, wire, field, forward, backward)


def field_kernel(lower_ref, upper_ref, out_ref):
    blank = jnp.zeros((1, lower_ref.shape[-1]), jnp.float32)
    lower = jnp.concatenate([lower_ref[...], blank], axis=0).astype(jnp.bfloat16)
    upper = jnp.concatenate([upper_ref[...], blank], axis=0).astype(jnp.bfloat16)
    once = jnp.concatenate([lower, lower, upper, upper], axis=0)
    out_ref[...] = jnp.concatenate([once, once], axis=0).T.reshape(PB, GRID, 128)


def field_call(potential):
    lanes = PB * GRID
    return pl.pallas_call(
        field_kernel,
        grid=(PAIRS // PB,),
        in_specs=[
            pl.BlockSpec((PLANES, lanes), lambda i: (0, i)),
            pl.BlockSpec((PLANES, lanes), lambda i: (0, i + PAIRS // PB)),
        ],
        out_specs=pl.BlockSpec((PB, GRID, 128), lambda i: (i, 0, 0)),
        out_shape=jax.ShapeDtypeStruct((PAIRS, GRID, 128), jnp.bfloat16),
        compiler_params=pltpu.CompilerParams(vmem_limit_bytes=60 * MIB),
        cost_estimate=pl.CostEstimate(flops=0, bytes_accessed=18_000_000, transcendentals=0),
        name="field",
    )(potential, potential)


def local(orbitals, potential, stick_column, column_slot):
    z_forward, z_backward, forward, backward = (jnp.asarray(table) for table in tables())
    live_all = stick_column >= 0
    own = lax.dynamic_slice_in_dim(stick_column, lax.axis_index("fft") * SLOTS, SLOTS)
    live = (own >= 0).astype(jnp.float32)[None, :]
    column_x, column_y = stick_column // GRID, stick_column % GRID
    box_x = jnp.where(column_x < GRID // 2, column_x + HALF, column_x - (GRID - HALF))
    box_y = jnp.where(column_y < GRID // 2, column_y + HALF, column_y - (GRID - HALF))
    place = jnp.where(live_all, box_y * BOX + box_x, ROWS)
    count = (jnp.sum(live_all.reshape(GROUPS, SLOTS).astype(jnp.int32), axis=1) + 127) // 128
    upper = (live_all & (box_y >= HALF)).astype(jnp.float32).reshape(GROUPS * SLOTS // 128, 128)
    me = lax.axis_index("band").astype(jnp.int32)[None]
    core = me % 2

    wire, kept, given = z_forward_call(core, orbitals.transpose(0, 2, 1), live, z_forward)
    incoming = lax.all_to_all(wire.reshape(GROUPS, 64, SLOTS), "fft", split_axis=0, concat_axis=0, tiled=True)
    shares, potential = spread_blocks(kept, given, potential)
    field = field_call(potential)
    incoming, field, place, count, upper, *shares = lax.optimization_barrier(
        (incoming, field, place, count, upper, *shares)
    )
    left = lax.all_to_all(twofold_call(incoming), "band", split_axis=0, concat_axis=0, tiled=True)
    left = left.reshape(8, 4, 2, 2, 16, SLOTS)
    outgoing, kept, given, *sides = plane_call(me, place, count, upper, incoming, field, forward, backward)
    piece = (1, 2, 2, 2, 16, SLOTS)
    sides = [side.reshape(piece) for side in sides]
    arrived = [moved(side, shift, other) for side, (shift, other) in zip(sides, ((1, 0), (1, 1), (3, 0), (3, 1)))]
    kept, got = kept.reshape(2, 2, 2, 2, 16, SLOTS), moved(given.reshape(2, 2, 2, 2, 16, SLOTS), 0, 1)
    returned = lax.all_to_all(outgoing, "fft", split_axis=0, concat_axis=0, tiled=True)
    products = gram_call(overlap_kernel, me, [(share, 2, 0, 0) for share in shares], (512, 512), "overlap")
    lefts = [(left, 8, 0, 0), (left, 8, 0, 2)]
    nears = [(kept, 1, 0, 0), (got, 1, 0, 0), (kept, 1, 1, 0), (got, 1, 1, 0)]
    products += gram_call(near_kernel, me, lefts + nears, (512, 128), "near")
    products += gram_call(next_kernel, me, lefts[:1] + [(side, 1, 0, 0) for side in arrived], (512, 256), "next")
    applied = z_backward_call(returned.reshape(GROUPS, 2, 2, ZPAD, SLOTS), live, z_backward)
    products, _ = summed(products, "band", (1, 2, 4))
    products, _ = summed(products, "fft", (1, 2))
    products, applied = summed(products, "fft", (4,), applied)
    products, _ = summed(products, "fft", (8,))
    products = products * (1.0 / (2.0 * STICKS * GRID))
    products = products[:, :64].reshape(16, 4, 16).transpose(1, 0, 2)
    return (applied.transpose(0, 2, 1), products[0:2], products[2:4])


def solution(mesh):
    return jax.shard_map(
        local,
        mesh=mesh,
        in_specs=(P("band", "fft", None), P("fft", None), P(), P()),
        out_specs=(P("band", "fft", None), P(), P()),
        check_vma=False,
    )
```
